256 devices in a mesh: tile: 32 (over x, z_lo, core), lev: 8 (over y, z_hi).
Axes of the slice: x: 4, y: 4, z: 8 (z_hi: 2, z_lo: 4; z = z_hi * 4 + z_lo), core: 2. Of those that a mesh axis runs over, the one named last changes fastest.
Arguments:
- ensemble: bfloat16 [80, 48, 32768], P(None, 'lev', 'tile'), may hold values from -6 to 6
- perturbed: float32 [8, 80, 256], replicated, may hold values from -6 to 6
- factor: float32 [8, 256, 256], replicated, may hold values from -0.04 to 0.32
- obs_tile: int32 [8, 256], replicated, may hold values from 0 to 31, as said below
- obs_column: int32 [8, 256], replicated, may hold values from 0 to 1023
- obs_level: int32 [8, 256], replicated, may hold values from 0 to 47
Outputs:
- posterior: bfloat16 [80, 48, 32768], P(None, 'lev', 'tile')
The draws below stay inside these ranges and needn't reach their ends.
Inputs may be any that keep to these rules, and one draw needn't show every extreme that they name: `obs_tile`: within each batch the owner tiles never fall; the first observation of a batch lies on tile 0 and the last on tile 32 - 1.
All inputs are finite; a program needn't handle non-finite values.
Results may differ from the reference program's by a relative error of at most 0.0033.
Values sent between devices are 32-bit elements; how exact they have to be, the bound alone decides.
A program may use at most 128 MiB of HBM per device.

```python
import jax
import jax.numpy as jnp
from jax import lax

MEMBERS = 80
OBS = 256
NB = 8
COLS = 1024
TILES = 32
LEVELS = 48
COLUMNS = 32768
RADIUS = 2560
VREACH = 12


def draw_factor(key, part):
    key = jax.random.fold_in(key, 11)
    first, second = jax.random.split(key)
    diagonal = jax.random.uniform(first, (NB, OBS), jnp.float32, 0.2, 0.32)
    offdiag = jax.random.normal(second, (NB, OBS, OBS), jnp.float32) * (0.14 / OBS ** 0.5)
    offdiag = jnp.clip(offdiag, -0.04, 0.04)
    identity = jnp.eye(OBS, dtype=jnp.float32)
    return offdiag * (1.0 - identity) + diagonal[:, :, None] * identity


def draw_obs_tile(key, part):
    key = jax.random.fold_in(key, 7)
    ticket = jax.random.randint(key, (NB, OBS), 0, 4096)
    tiles_drawn = ticket * ticket * TILES // 16777216
    tiles_drawn = jnp.sort(tiles_drawn, axis=1)
    tiles_drawn = tiles_drawn.at[:, 0].set(0).at[:, OBS - 1].set(TILES - 1)
    return tiles_drawn.astype(jnp.int32)


def with_ends(drawn, own_key, low, top_value):
    dims = drawn.shape
    spot = [jax.random.randint(jax.random.fold_in(own_key, axis), (), 0, dims[axis]) for axis in range(len(dims))]
    drawn = drawn.at[tuple(spot)].set(low)
    longest = dims.index(max(dims))
    spot[longest] = (spot[longest] + 1) % dims[longest]
    return drawn.at[tuple(spot)].set(top_value)


def block_scale(rng, shape, shards, low, largest):
    def one(position, shards_of):
        steps = jax.random.uniform(jax.random.fold_in(jax.random.fold_in(rng, 6), position), (shards_of,), jnp.float32, low / len(shards), largest / len(shards))
        return jnp.repeat(jnp.exp(steps), shape[position] // shards_of).reshape((-1,) + (1,) * (len(shape) - position - 1))

    loudness = one(*shards[0])
    for cut in shards[1:]:
        loudness = loudness * one(*cut)
    return loudness


def bell_draw(stream_key, extent, scale, reach, pieces=(), kind=jnp.bfloat16):
    result = scale * jax.random.normal(stream_key, extent, jnp.float32)
    if pieces:
        result = result * block_scale(stream_key, extent, pieces, -0.22, 0.18)
    return jnp.clip(result, -reach, reach).astype(kind)


def setup_inputs(seed: int = 0) -> dict:
    key_list = jax.random.split(jax.random.key(seed), 7)
    return {
        "ensemble": bell_draw(key_list[0], (MEMBERS, LEVELS, COLUMNS), 1.0, 6.0, ((1, 8), (2, 32))),
        "perturbed": bell_draw(key_list[1], (NB, MEMBERS, OBS), 1.0, 6.0, (), jnp.float32),
        "factor": draw_factor(jax.random.fold_in(key_list[6], 71), 0),
        "obs_tile": draw_obs_tile(jax.random.fold_in(key_list[6], 71), 0),
        "obs_column": with_ends(jax.random.randint(key_list[4], (NB, OBS), 0, COLS), jax.random.fold_in(key_list[4], 1), 0, COLS - 1).astype(jnp.int32),
        "obs_level": with_ends(jax.random.randint(key_list[5], (NB, OBS), 0, LEVELS), jax.random.fold_in(key_list[5], 1), 0, LEVELS - 1).astype(jnp.int32),
    }


def horizontal(obs_gcol, positions, columns):
    distance = jnp.abs(positions[None, :] - obs_gcol[:, None])
    distance = jnp.minimum(distance, columns - distance)
    return jnp.maximum(0.0, 1.0 - distance.astype(jnp.float32) / RADIUS)


def vertical(lev_obs, level_arr):
    inverse = 1.0 / (MEMBERS - 1)
    reach_sq = float(VREACH * VREACH)
    offset = (lev_obs[:, None] - level_arr[None, :]).astype(jnp.float32)
    return reach_sq / (reach_sq + offset * offset) * inverse


def spread(values):
    return (values - jnp.mean(values, axis=0, keepdims=True)).astype(jnp.bfloat16)


def weights(priors, observed, inv_factor):
    innovation = observed - priors
    half_step = jnp.dot(innovation, inv_factor.T, precision=lax.Precision.HIGHEST)
    return jnp.dot(half_step, inv_factor, precision=lax.Precision.HIGHEST).astype(jnp.bfloat16)


def level_update(dev_level, prior_dev, obs_weight, horiz_taper, vert_weight):
    covar = lax.dot_general(prior_dev, dev_level, (((0,), (0,)), ((), ())), preferred_element_type=jnp.float32)
    tapered = (covar * horiz_taper * vert_weight).astype(jnp.bfloat16)
    return jnp.dot(obs_weight, tapered, preferred_element_type=jnp.float32)


def reference(ensemble, perturbed, factor, obs_tile, obs_column, obs_level):
    current = ensemble.astype(jnp.float32)
    positions = jnp.arange(COLUMNS, dtype=jnp.int32)
    for batch in range(NB):
        obs_gcol = (obs_tile[batch] * COLS + obs_column[batch]).astype(jnp.int32)
        flat_index = (obs_level[batch] * COLUMNS + obs_gcol).astype(jnp.int32)
        priors = jnp.take(current.reshape(MEMBERS, LEVELS * COLUMNS), flat_index, axis=1)
        prior_dev = spread(priors)
        obs_weight = weights(priors, perturbed[batch], factor[batch])
        state_dev = spread(current)
        horiz_taper = horizontal(obs_gcol, positions, COLUMNS)
        lev_obs = obs_level[batch]

        def one_level(level, accumulated):
            dev_level = lax.dynamic_index_in_dim(state_dev, level, 1, keepdims=False)
            vert_weight = vertical(lev_obs, jnp.reshape(level, (1,)).astype(jnp.int32))
            update = level_update(dev_level, prior_dev, obs_weight, horiz_taper, vert_weight)
            return lax.dynamic_update_index_in_dim(accumulated, update, level, 1)

        increment = lax.fori_loop(0, LEVELS, one_level, jnp.zeros(current.shape, jnp.float32))
        current = current + increment
    return current.astype(jnp.bfloat16)
```

```python
import jax
import jax.numpy as jnp
from jax import lax
from jax.experimental import pallas as pl
from jax.experimental.pallas import tpu as pltpu
from jax.sharding import PartitionSpec as P

MEMBERS = 80
OBS = 256
NB = 8
COLS = 1024
LEV = 6
COLUMNS = 32768
RADIUS = 2560
VREACH = 12

HALF = 80
PIECE = 5
PLANE = 16
DEPTH = 8

F32 = jnp.float32
BF16 = jnp.bfloat16


def down(row):
    return jnp.broadcast_to(row, (128, OBS)).T


def inverse_of(value):
    rough = pl.reciprocal(value, approx=True)
    return rough * (2.0 - value * rough)


def exchange_kernel(ens_h, tile_h, col_h, lev_h, fac_h, *refs):
    (obs_out, ghi_out, glo_out), refs = refs[:3], refs[3:]
    taper_out, refs = refs[:NB - 1], refs[NB - 1:]
    exchange_body((ens_h, tile_h, col_h, lev_h, fac_h), obs_out, ghi_out, glo_out, taper_out, *refs)


def exchange_body(given, obs_out, ghi_out, glo_out, taper_out,
                  ens, tile_r, col_r, lev_r, fac, load, buf, r0, s0, r1, s1, r2, s2, full,
                  send0, recv0, send1, recv1, send2, recv2, send3, recv3, send4, recv4):
    t = lax.axis_index("tile")
    l = lax.axis_index("lev")
    core = t % 2
    z_lo = (t // 2) % 4
    x = t // 8
    y = l // 2
    z_hi = l % 2
    plane = x * 4 + y
    z = z_hi * 4 + z_lo

    def plane_peer(d):
        j = (plane + d) % PLANE
        return j, {"tile": (j // 4) * 8 + z_lo * 2 + core, "lev": (j % 4) * 2 + z_hi}

    def depth_peer(d):
        j = (z + d) % DEPTH
        return j, {"tile": x * 8 + (j % 4) * 2 + core, "lev": y * 2 + j // 4}

    loads = [pltpu.make_async_copy(src, dst, load.at[i])
             for i, (src, dst) in enumerate(zip(given, (ens, tile_r, col_r, lev_r, fac)))]
    for i in (1, 2, 3, 0, 4):
        loads[i].start()

    mate = {"tile": t + 1 - 2 * core, "lev": l}
    peers = [mate] + [plane_peer(d)[1] for d in range(1, PLANE)]
    peers += [depth_peer(d)[1] for d in range(1, DEPTH)]
    barrier = pltpu.get_barrier_semaphore()
    for peer in peers:
        pl.semaphore_signal(barrier, inc=1, device_id=peer, device_id_type=pl.DeviceIdType.MESH)

    for i in range(4):
        loads[i].wait()

    def pick(b, carry):
        owned = tile_r[pl.ds(b, 1), :] == t
        column = jnp.where(owned, col_r[pl.ds(b, 1), :], -1)
        level = lev_r[pl.ds(b, 1), :] - l * LEV
        rows = lax.broadcasted_iota(jnp.int32, (COLS, OBS), 0)
        onehot = jnp.where(rows == column, 1.0, 0.0).astype(BF16)
        got = jnp.dot(ens[...], onehot, preferred_element_type=F32)
        total = jnp.zeros((MEMBERS, OBS), F32)
        for v in range(LEV):
            total = total + jnp.where(level == v, got[v * MEMBERS:(v + 1) * MEMBERS], 0.0)
        for h in range(2):
            for mb in range(10):
                buf[b * 20 + h * 10 + mb] = total[mb * 8:mb * 8 + 8, h * 128:h * 128 + 128]
        return carry
    lax.fori_loop(0, NB, pick, 0, unroll=2)

    pl.semaphore_wait(barrier, len(peers))

    order = list(range(1, PLANE)) + [0]
    pair = {}
    for d in order:
        j, _ = plane_peer(d)
        c = pltpu.make_async_remote_copy(
            src_ref=buf.at[pl.ds((1 - core) * HALF + j * PIECE, PIECE)],
            dst_ref=r0.at[j], send_sem=send0.at[d], recv_sem=recv0.at[d],
            device_id=mate, device_id_type=pl.DeviceIdType.MESH)
        c.start()
        pair[d] = c
    spread_out = {}
    for d in order:
        j, peer = plane_peer(d)
        pair[d].wait_recv()
        s0[j] = buf[pl.ds(core * HALF + j * PIECE, PIECE)] + r0[j]
        if d:
            c = pltpu.make_async_remote_copy(
                src_ref=s0.at[j], dst_ref=r1.at[d], send_sem=send1.at[d], recv_sem=recv1.at[d],
                device_id=peer, device_id_type=pl.DeviceIdType.MESH)
            c.start()
            spread_out[d] = c

    loads[4].wait()

    def gram(b, carry):
        f = fac[b]
        g = lax.dot_general(f, f, (((0,), (0,)), ((), ())), precision=lax.Precision.HIGHEST,
                            preferred_element_type=F32)
        hi = g.astype(BF16)
        ghi_out[b] = hi
        glo_out[b] = (g - hi.astype(F32)).astype(BF16)
        return carry
    lax.fori_loop(0, NB, gram, 0)

    reach_sq = float(VREACH * VREACH)
    inverse = 1.0 / (MEMBERS - 1)

    def tapers_of(b):
        gcol_d = down((tile_r[b:b + 1, :] * COLS + col_r[b:b + 1, :]).astype(F32))
        level_d = down(lev_r[b:b + 1, :].astype(F32))

        def later(b2, carry):
            g2 = (tile_r[pl.ds(b2, 1), :] * COLS + col_r[pl.ds(b2, 1), :]).astype(F32)
            l2 = lev_r[pl.ds(b2, 1), :].astype(F32)
            for h in range(2):
                cut = slice(h * 128, h * 128 + 128)
                dist = jnp.abs(gcol_d - g2[:, cut])
                dist = jnp.minimum(dist, COLUMNS - dist)
                taper = jnp.maximum(0.0, 1.0 - dist * (1.0 / RADIUS))
                off = level_d - l2[:, cut]
                vert = (reach_sq * inverse) * inverse_of(reach_sq + off * off)
                place = pl.multiple_of((b2 - b - 1) * OBS + h * 128, 128)
                taper_out[b][:, pl.ds(place, 128)] = taper * vert
            return carry
        lax.fori_loop(b + 1, NB, later, 0)

    total = s0[plane]
    for d in range(1, PLANE):
        spread_out[d].wait_recv()
        total = total + r1[d]
    s1[...] = total
    along = {}
    for d in range(1, DEPTH):
        _, peer = depth_peer(d)
        c = pltpu.make_async_remote_copy(
            src_ref=s1, dst_ref=r2.at[d], send_sem=send2.at[d], recv_sem=recv2.at[d],
            device_id=peer, device_id_type=pl.DeviceIdType.MESH)
        c.start()
        along[d] = c
    for b in range(3):
        tapers_of(b)
    for d in range(1, DEPTH):
        along[d].wait_recv()
        total = total + r2[d]
    s2[...] = total
    full[pl.ds(core * HALF + plane * PIECE, PIECE)] = total

    gathered = {}
    for d in range(1, PLANE):
        _, peer = plane_peer(d)
        c = pltpu.make_async_remote_copy(
            src_ref=s2, dst_ref=full.at[pl.ds(core * HALF + plane * PIECE, PIECE)],
            send_sem=send3.at[d], recv_sem=recv3.at[d],
            device_id=peer, device_id_type=pl.DeviceIdType.MESH)
        c.start()
        gathered[d] = c
    for b in range(3, NB - 1):
        tapers_of(b)
    passed = {}
    for d in range(PLANE):
        j = (plane - d + PLANE) % PLANE
        if d:
            gathered[d].wait_recv()
        part = full.at[pl.ds(core * HALF + j * PIECE, PIECE)]
        c = pltpu.make_async_remote_copy(
            src_ref=part, dst_ref=part, send_sem=send4.at[d], recv_sem=recv4.at[d],
            device_id=mate, device_id_type=pl.DeviceIdType.MESH)
        c.start()
        passed[d] = c
    for d in range(PLANE):
        passed[d].wait_recv()

    def unpack(cb, carry):
        for mb in range(10):
            obs_out[mb * 8:mb * 8 + 8, pl.ds(pl.multiple_of(cb * 128, 128), 128)] = full[cb * 10 + mb]
        return carry
    lax.fori_loop(0, 16, unpack, 0)

    for d in range(PLANE):
        pair[d].wait_send()
        passed[d].wait_send()
        if d:
            spread_out[d].wait_send()
            gathered[d].wait_send()
        if 0 < d < DEPTH:
            along[d].wait_send()


def exchange(ensemble, obs_tile, obs_column, obs_level, factor):
    vmem = pl.BlockSpec(memory_space=pltpu.VMEM)
    dma = pltpu.SemaphoreType.DMA
    piece = (PIECE, 8, 128)
    return pl.pallas_call(
        exchange_kernel,
        out_shape=(
            jax.ShapeDtypeStruct((MEMBERS, NB * OBS), F32),
            jax.ShapeDtypeStruct((NB, OBS, OBS), BF16),
            jax.ShapeDtypeStruct((NB, OBS, OBS), BF16),
        ) + tuple(jax.ShapeDtypeStruct((OBS, (NB - 1 - b) * OBS), F32) for b in range(NB - 1)),
        in_specs=[pl.BlockSpec(memory_space=pltpu.HBM)] * 5,
        out_specs=(vmem,) * (NB + 2),
        scratch_shapes=[
            pltpu.VMEM((LEV * MEMBERS, COLS), BF16),
            pltpu.VMEM((NB, OBS), jnp.int32),
            pltpu.VMEM((NB, OBS), jnp.int32),
            pltpu.VMEM((NB, OBS), jnp.int32),
            pltpu.VMEM((NB, OBS, OBS), F32),
            dma((5,)),
            pltpu.VMEM((2 * HALF, 8, 128), F32),
            pltpu.VMEM((PLANE,) + piece, F32),
            pltpu.VMEM((PLANE,) + piece, F32),
            pltpu.VMEM((PLANE,) + piece, F32),
            pltpu.VMEM(piece, F32),
            pltpu.VMEM((DEPTH,) + piece, F32),
            pltpu.VMEM(piece, F32),
            pltpu.VMEM((2 * HALF, 8, 128), F32),
            dma((PLANE,)), dma((PLANE,)), dma((PLANE,)), dma((PLANE,)),
            dma((DEPTH,)), dma((DEPTH,)),
            dma((PLANE,)), dma((PLANE,)), dma((PLANE,)), dma((PLANE,)),
        ],
        compiler_params=pltpu.CompilerParams(
            collective_id=0, has_side_effects=True, vmem_limit_bytes=14 * 1024 * 1024),
        name="exchange",
    )(ensemble, obs_tile, obs_column, obs_level, factor)


def centred(values):
    return values - jnp.sum(values, axis=0, keepdims=True) * (1.0 / MEMBERS)


def update_kernel(x_ref, obs_ref, pert, ghi, glo, tile_r, col_r, lev_r, *refs):
    tapers, (out, state, aug, horiz) = refs[:NB - 1], refs[NB - 1:]
    t = lax.axis_index("tile")
    first = lax.axis_index("lev") * LEV
    state[...] = x_ref[...].astype(F32)
    aug[...] = obs_ref[...]
    reach_sq = float(VREACH * VREACH)
    inverse = 1.0 / (MEMBERS - 1)
    lanes = lax.broadcasted_iota(jnp.int32, (OBS, 128), 1)

    for b in range(NB):
        priors = aug[:, b * OBS:(b + 1) * OBS]
        prior_dev = centred(priors)
        innovation = pert[b] - priors
        in_hi = innovation.astype(BF16)
        in_lo = (innovation - in_hi.astype(F32)).astype(BF16)
        g_hi = ghi[b]
        weight = (jnp.dot(in_hi, g_hi, preferred_element_type=F32)
                  + jnp.dot(in_lo, g_hi, preferred_element_type=F32)
                  + jnp.dot(in_hi, glo[b], preferred_element_type=F32)).astype(BF16)
        dev_t = prior_dev.T
        if b + 1 < NB:
            rest = slice((b + 1) * OBS, NB * OBS)
            values = aug[:, rest]
            covar = jnp.dot(dev_t.astype(BF16), centred(values).astype(BF16), preferred_element_type=F32)
            tapered = (covar * tapers[b][...]).astype(BF16)
            aug[:, rest] = values + jnp.dot(weight, tapered, preferred_element_type=F32)

        gcol_d = down((tile_r[b:b + 1, :] * COLS + col_r[b:b + 1, :]).astype(F32))
        level_d = down(lev_r[b:b + 1, :].astype(F32))
        for q in range(COLS // 128):
            dist = jnp.abs(gcol_d - (t * COLS + q * 128 + lanes).astype(F32))
            dist = jnp.minimum(dist, COLUMNS - dist)
            horiz[b % 2, :, q * 128:q * 128 + 128] = jnp.maximum(0.0, 1.0 - dist * (1.0 / RADIUS))

        def first_dot(v):
            off = level_d[:, 0:MEMBERS] - (first + v).astype(F32)
            vert = (reach_sq * inverse) / (reach_sq + off * off)
            dev_v = (dev_t * vert).astype(BF16)
            values = state[v * MEMBERS:(v + 1) * MEMBERS, :]
            return jnp.dot(dev_v, centred(values).astype(BF16), preferred_element_type=F32)

        ahead = first_dot(0)
        for v in range(LEV):
            covar = ahead
            if v + 1 < LEV:
                ahead = first_dot(v + 1)
            rows = slice(v * MEMBERS, (v + 1) * MEMBERS)
            tapered = (covar * horiz[b % 2]).astype(BF16)
            values = state[rows, :] + jnp.dot(weight, tapered, preferred_element_type=F32)
            if b + 1 < NB:
                state[rows, :] = values
            else:
                out[rows, :] = values.astype(BF16)


def update(x, obs, perturbed, ghi, glo, obs_tile, obs_column, obs_level, tapers):
    vmem = pl.BlockSpec(memory_space=pltpu.VMEM)
    return pl.pallas_call(
        update_kernel,
        out_shape=jax.ShapeDtypeStruct((LEV * MEMBERS, COLS), BF16),
        in_specs=[vmem] * (8 + NB - 1),
        out_specs=vmem,
        scratch_shapes=[
            pltpu.VMEM((LEV * MEMBERS, COLS), F32),
            pltpu.VMEM((MEMBERS, NB * OBS), F32),
            pltpu.VMEM((2, OBS, COLS), F32),
        ],
        compiler_params=pltpu.CompilerParams(vmem_limit_bytes=28 * 1024 * 1024),
        name="update",
    )(x, obs, perturbed, ghi, glo, obs_tile, obs_column, obs_level, *tapers)


def per_device(ensemble, perturbed, factor, obs_tile, obs_column, obs_level):
    x = ensemble.transpose(1, 0, 2).reshape(LEV * MEMBERS, COLS)
    obs, ghi, glo, *tapers = exchange(x, obs_tile, obs_column, obs_level, factor)
    posterior = update(x, obs, perturbed, ghi, glo, obs_tile, obs_column, obs_level, tapers)
    return posterior.reshape(LEV, MEMBERS, COLS).transpose(1, 0, 2)


def solution(mesh):
    return jax.shard_map(
        per_device,
        mesh=mesh,
        in_specs=(P(None, "lev", "tile"), P(), P(), P(), P(), P()),
        out_specs=P(None, "lev", "tile"),
        check_vma=False,
    )
```

```python
import jax
import jax.numpy as jnp
from jax import lax
from jax.experimental import pallas as pl
from jax.experimental.pallas import tpu as pltpu
from jax.sharding import PartitionSpec as P

MEMBERS = 80
OBS = 256
NB = 8
COLS = 1024
LEV = 6
COLUMNS = 32768
RADIUS = 2560
VREACH = 12
TILES = 32
NEAR = -(-RADIUS // COLS)

HALF = 80
PIECE = 5
PLANE = 16
DEPTH = 8

F32 = jnp.float32
BF16 = jnp.bfloat16


def down(row):
    return jnp.broadcast_to(row, (128, OBS)).T


def inverse_of(value):
    rough = pl.reciprocal(value, approx=True)
    return rough * (2.0 - value * rough)


def exchange_kernel(ens_h, tile_h, col_h, lev_h, fac_h, *refs):
    (obs_out, ghi_out, glo_out), refs = refs[:3], refs[3:]
    taper_out, refs = refs[:NB - 1], refs[NB - 1:]
    exchange_body((ens_h, tile_h, col_h, lev_h, fac_h), obs_out, ghi_out, glo_out, taper_out, *refs)


def exchange_body(given, obs_out, ghi_out, glo_out, taper_out,
                  ens, tile_r, col_r, lev_r, fac, load, buf, r0, s0, r1, s1, r2, s2, full,
                  send0, recv0, send1, recv1, send2, recv2, send3, recv3, send4, recv4):
    t = lax.axis_index("tile")
    l = lax.axis_index("lev")
    core = t % 2
    z_lo = (t // 2) % 4
    x = t // 8
    y = l // 2
    z_hi = l % 2
    plane = x * 4 + y
    z = z_hi * 4 + z_lo

    def plane_peer(d):
        j = (plane + d) % PLANE
        return j, {"tile": (j // 4) * 8 + z_lo * 2 + core, "lev": (j % 4) * 2 + z_hi}

    def depth_peer(d):
        j = (z + d) % DEPTH
        return j, {"tile": x * 8 + (j % 4) * 2 + core, "lev": y * 2 + j // 4}

    loads = [pltpu.make_async_copy(src, dst, load.at[i])
             for i, (src, dst) in enumerate(zip(given, (ens, tile_r, col_r, lev_r, fac)))]
    for i in (1, 2, 3, 0, 4):
        loads[i].start()

    mate = {"tile": t + 1 - 2 * core, "lev": l}
    peers = [mate] + [plane_peer(d)[1] for d in range(1, PLANE)]
    peers += [depth_peer(d)[1] for d in range(1, DEPTH)]
    barrier = pltpu.get_barrier_semaphore()
    for peer in peers:
        pl.semaphore_signal(barrier, inc=1, device_id=peer, device_id_type=pl.DeviceIdType.MESH)

    for i in range(4):
        loads[i].wait()

    def pick(b, carry):
        owned = tile_r[pl.ds(b, 1), :] == t
        column = jnp.where(owned, col_r[pl.ds(b, 1), :], -1)
        level = lev_r[pl.ds(b, 1), :] - l * LEV
        rows = lax.broadcasted_iota(jnp.int32, (COLS, OBS), 0)
        onehot = jnp.where(rows == column, 1.0, 0.0).astype(BF16)
        got = jnp.dot(ens[...], onehot, preferred_element_type=F32)
        total = jnp.zeros((MEMBERS, OBS), F32)
        for v in range(LEV):
            total = total + jnp.where(level == v, got[v * MEMBERS:(v + 1) * MEMBERS], 0.0)
        for h in range(2):
            for mb in range(10):
                buf[b * 20 + h * 10 + mb] = total[mb * 8:mb * 8 + 8, h * 128:h * 128 + 128]
        return carry

    def pair_copy(j):
        return pltpu.make_async_remote_copy(
            src_ref=buf.at[pl.ds((1 - core) * HALF + j * PIECE, PIECE)],
            dst_ref=r0.at[j], send_sem=send0.at[j], recv_sem=recv0.at[j],
            device_id=mate, device_id_type=pl.DeviceIdType.MESH)

    for step in range(4):
        from_batch = (step * 2 + 4 * (1 - core)) % NB
        lax.fori_loop(0, 2, lambda i, c, from_batch=from_batch: pick(from_batch + i, c), 0, unroll=True)
        if step == 0:
            pl.semaphore_wait(barrier, len(peers))
        if step < 2:
            for j in range(step * 8, step * 8 + 8):
                pair_copy(j).start()

    order = list(range(1, PLANE)) + [0]
    spread_out = {}
    for d in order:
        j, peer = plane_peer(d)
        pair_copy(j).wait_recv()
        s0[j] = buf[pl.ds(core * HALF + j * PIECE, PIECE)] + r0[j]
        if d:
            c = pltpu.make_async_remote_copy(
                src_ref=s0.at[j], dst_ref=r1.at[d], send_sem=send1.at[d], recv_sem=recv1.at[d],
                device_id=peer, device_id_type=pl.DeviceIdType.MESH)
            c.start()
            spread_out[d] = c

    loads[4].wait()

    def gram(b, carry):
        f = fac[b]
        g = lax.dot_general(f, f, (((0,), (0,)), ((), ())), precision=lax.Precision.HIGHEST,
                            preferred_element_type=F32)
        hi = g.astype(BF16)
        ghi_out[b] = hi
        glo_out[b] = (g - hi.astype(F32)).astype(BF16)
        return carry
    lax.fori_loop(0, NB, gram, 0)

    reach_sq = float(VREACH * VREACH)
    inverse = 1.0 / (MEMBERS - 1)

    def tapers_of(b):
        gcol_d = down((tile_r[b:b + 1, :] * COLS + col_r[b:b + 1, :]).astype(F32))
        level_d = down(lev_r[b:b + 1, :].astype(F32))

        def later(b2, carry):
            g2 = (tile_r[pl.ds(b2, 1), :] * COLS + col_r[pl.ds(b2, 1), :]).astype(F32)
            l2 = lev_r[pl.ds(b2, 1), :].astype(F32)
            for h in range(2):
                cut = slice(h * 128, h * 128 + 128)
                dist = jnp.abs(gcol_d - g2[:, cut])
                dist = jnp.minimum(dist, COLUMNS - dist)
                taper = jnp.maximum(0.0, 1.0 - dist * (1.0 / RADIUS))
                off = level_d - l2[:, cut]
                vert = (reach_sq * inverse) * inverse_of(reach_sq + off * off)
                place = pl.multiple_of((b2 - b - 1) * OBS + h * 128, 128)
                taper_out[b][:, pl.ds(place, 128)] = taper * vert
            return carry
        lax.fori_loop(b + 1, NB, later, 0)

    total = s0[plane]
    for d in range(1, PLANE):
        spread_out[d].wait_recv()
        total = total + r1[d]
    s1[...] = total
    along = {}
    for d in range(1, DEPTH):
        _, peer = depth_peer(d)
        c = pltpu.make_async_remote_copy(
            src_ref=s1, dst_ref=r2.at[d], send_sem=send2.at[d], recv_sem=recv2.at[d],
            device_id=peer, device_id_type=pl.DeviceIdType.MESH)
        c.start()
        along[d] = c
    for b in range(3):
        tapers_of(b)
    for d in range(1, DEPTH):
        along[d].wait_recv()
        total = total + r2[d]
    s2[...] = total
    full[pl.ds(core * HALF + plane * PIECE, PIECE)] = total

    gathered = {}
    for d in range(1, PLANE):
        _, peer = plane_peer(d)
        c = pltpu.make_async_remote_copy(
            src_ref=s2, dst_ref=full.at[pl.ds(core * HALF + plane * PIECE, PIECE)],
            send_sem=send3.at[d], recv_sem=recv3.at[d],
            device_id=peer, device_id_type=pl.DeviceIdType.MESH)
        c.start()
        gathered[d] = c
    for b in range(3, NB - 1):
        tapers_of(b)
    passed = {}
    for d in range(PLANE):
        j = (plane - d + PLANE) % PLANE
        if d:
            gathered[d].wait_recv()
        part = full.at[pl.ds(core * HALF + j * PIECE, PIECE)]
        c = pltpu.make_async_remote_copy(
            src_ref=part, dst_ref=part, send_sem=send4.at[d], recv_sem=recv4.at[d],
            device_id=mate, device_id_type=pl.DeviceIdType.MESH)
        c.start()
        passed[d] = c
    for d in range(PLANE):
        passed[d].wait_recv()

    def unpack(cb, carry):
        for mb in range(10):
            obs_out[mb * 8:mb * 8 + 8, pl.ds(pl.multiple_of(cb * 128, 128), 128)] = full[cb * 10 + mb]
        return carry
    lax.fori_loop(0, 16, unpack, 0)

    for d in range(PLANE):
        pair_copy(d).wait_send()
        passed[d].wait_send()
        if d:
            spread_out[d].wait_send()
            gathered[d].wait_send()
        if 0 < d < DEPTH:
            along[d].wait_send()


def exchange(ensemble, obs_tile, obs_column, obs_level, factor):
    vmem = pl.BlockSpec(memory_space=pltpu.VMEM)
    dma = pltpu.SemaphoreType.DMA
    piece = (PIECE, 8, 128)
    return pl.pallas_call(
        exchange_kernel,
        out_shape=(
            jax.ShapeDtypeStruct((MEMBERS, NB * OBS), F32),
            jax.ShapeDtypeStruct((NB, OBS, OBS), BF16),
            jax.ShapeDtypeStruct((NB, OBS, OBS), BF16),
        ) + tuple(jax.ShapeDtypeStruct((OBS, (NB - 1 - b) * OBS), F32) for b in range(NB - 1)),
        in_specs=[pl.BlockSpec(memory_space=pltpu.HBM)] * 5,
        out_specs=(vmem,) * (NB + 2),
        scratch_shapes=[
            pltpu.VMEM((LEV * MEMBERS, COLS), BF16),
            pltpu.VMEM((NB, OBS), jnp.int32),
            pltpu.VMEM((NB, OBS), jnp.int32),
            pltpu.VMEM((NB, OBS), jnp.int32),
            pltpu.VMEM((NB, OBS, OBS), F32),
            dma((5,)),
            pltpu.VMEM((2 * HALF, 8, 128), F32),
            pltpu.VMEM((PLANE,) + piece, F32),
            pltpu.VMEM((PLANE,) + piece, F32),
            pltpu.VMEM((PLANE,) + piece, F32),
            pltpu.VMEM(piece, F32),
            pltpu.VMEM((DEPTH,) + piece, F32),
            pltpu.VMEM(piece, F32),
            pltpu.VMEM((2 * HALF, 8, 128), F32),
            dma((PLANE,)), dma((PLANE,)), dma((PLANE,)), dma((PLANE,)),
            dma((DEPTH,)), dma((DEPTH,)),
            dma((PLANE,)), dma((PLANE,)), dma((PLANE,)), dma((PLANE,)),
        ],
        compiler_params=pltpu.CompilerParams(
            collective_id=0, has_side_effects=True, vmem_limit_bytes=14 * 1024 * 1024),
        name="exchange",
    )(*(pltpu.with_memory_space_constraint(a, pltpu.HBM)
        for a in (ensemble, obs_tile, obs_column, obs_level, factor)))


def centred(values):
    return values - jnp.sum(values, axis=0, keepdims=True) * (1.0 / MEMBERS)


def update_kernel(x_ref, obs_ref, pert, ghi, glo, tile_r, col_r, lev_r, *refs):
    tapers = refs[:NB - 1]
    out, state, aug, devs, weights, gcols, levels, horiz, counts = refs[NB - 1:]
    t = lax.axis_index("tile")
    first = lax.axis_index("lev") * LEV
    state[...] = x_ref[...].astype(F32)
    aug[...] = obs_ref[...]
    reach_sq = float(VREACH * VREACH)
    inverse = 1.0 / (MEMBERS - 1)

    low = (t + TILES - NEAR) % TILES
    turns = []
    for b in range(NB):
        owner = tile_r[b:b + 1, :]
        rel = owner - low
        rel = jnp.where(rel < 0, rel + TILES, rel)
        counts[b] = jnp.sum(jnp.where(rel < 2 * NEAR + 1, 1.0, 0.0)).astype(jnp.int32)
        skipped = jnp.sum(jnp.where(owner < low, 1.0, 0.0)).astype(jnp.int32)
        turns.append(lax.rem(OBS - skipped, OBS))

    for b in range(NB):
        priors = aug[:, b * OBS:(b + 1) * OBS]
        prior_dev = centred(priors)
        innovation = pert[b] - priors
        in_hi = innovation.astype(BF16)
        in_lo = (innovation - in_hi.astype(F32)).astype(BF16)
        g_hi = ghi[b]
        full_weight = (jnp.dot(in_hi, g_hi, preferred_element_type=F32)
                       + jnp.dot(in_lo, g_hi, preferred_element_type=F32)
                       + jnp.dot(in_hi, glo[b], preferred_element_type=F32))
        if b + 1 < NB:
            rest = slice((b + 1) * OBS, NB * OBS)
            values = aug[:, rest]
            covar = jnp.dot(prior_dev.T.astype(BF16), centred(values).astype(BF16),
                            preferred_element_type=F32)
            tapered = (covar * tapers[b][...]).astype(BF16)
            aug[:, rest] = values + jnp.dot(full_weight.astype(BF16), tapered,
                                            preferred_element_type=F32)
        devs[b] = pltpu.roll(prior_dev, turns[b], 1).T
        weights[b] = pltpu.roll(full_weight, turns[b], 1).astype(BF16)
        gcol = (tile_r[b:b + 1, :] * COLS + col_r[b:b + 1, :]).astype(F32)
        gcols[b] = pltpu.roll(jnp.broadcast_to(gcol, (128, OBS)), turns[b], 1).T
        lev = lev_r[b:b + 1, :].astype(F32)
        levels[b] = pltpu.roll(jnp.broadcast_to(lev, (128, OBS)), turns[b], 1).T

    def regress(b, width):
        lanes = lax.broadcasted_iota(jnp.int32, (width, 128), 1)
        gcol_d = gcols[b, 0:width]
        for q in range(COLS // 128):
            dist = jnp.abs(gcol_d - (t * COLS + q * 128 + lanes).astype(F32))
            dist = jnp.minimum(dist, COLUMNS - dist)
            horiz[0:width, q * 128:q * 128 + 128] = jnp.maximum(0.0, 1.0 - dist * (1.0 / RADIUS))
        weight = weights[b][:, 0:width]
        level_d = levels[b, 0:width, 0:MEMBERS]
        dev_t = devs[b, 0:width, :]

        def first_dot(v):
            off = level_d - (first + v).astype(F32)
            vert = (reach_sq * inverse) * inverse_of(reach_sq + off * off)
            values = state[v * MEMBERS:(v + 1) * MEMBERS, :]
            return jnp.dot((dev_t * vert).astype(BF16), centred(values).astype(BF16),
                           preferred_element_type=F32)

        ahead = first_dot(0)
        for v in range(LEV):
            covar = ahead
            if v + 1 < LEV:
                ahead = first_dot(v + 1)
            rows = slice(v * MEMBERS, (v + 1) * MEMBERS)
            tapered = (covar * horiz[0:width, :]).astype(BF16)
            state[rows, :] = state[rows, :] + jnp.dot(weight, tapered, preferred_element_type=F32)

    def batch(b, carry):
        near = counts[b]

        @pl.when(near <= OBS // 2)
        def _():
            regress(b, OBS // 2)

        @pl.when(near > OBS // 2)
        def _():
            regress(b, OBS)
        return carry
    lax.fori_loop(0, NB, batch, 0)
    out[...] = state[...].astype(BF16)


def update(x, obs, perturbed, ghi, glo, obs_tile, obs_column, obs_level, tapers):
    vmem = pl.BlockSpec(memory_space=pltpu.VMEM)
    return pl.pallas_call(
        update_kernel,
        out_shape=jax.ShapeDtypeStruct((LEV * MEMBERS, COLS), BF16),
        in_specs=[vmem] * (8 + NB - 1),
        out_specs=vmem,
        scratch_shapes=[
            pltpu.VMEM((LEV * MEMBERS, COLS), F32),
            pltpu.VMEM((MEMBERS, NB * OBS), F32),
            pltpu.VMEM((NB, OBS, MEMBERS), F32),
            pltpu.VMEM((NB, MEMBERS, OBS), BF16),
            pltpu.VMEM((NB, OBS, 128), F32),
            pltpu.VMEM((NB, OBS, 128), F32),
            pltpu.VMEM((OBS, COLS), F32),
            pltpu.SMEM((NB,), jnp.int32),
        ],
        compiler_params=pltpu.CompilerParams(vmem_limit_bytes=28 * 1024 * 1024),
        name="update",
    )(x, obs, perturbed, ghi, glo, obs_tile, obs_column, obs_level, *tapers)


def per_device(ensemble, perturbed, factor, obs_tile, obs_column, obs_level):
    x = ensemble.transpose(1, 0, 2).reshape(LEV * MEMBERS, COLS)
    obs, ghi, glo, *tapers = exchange(x, obs_tile, obs_column, obs_level, factor)
    posterior = update(x, obs, perturbed, ghi, glo, obs_tile, obs_column, obs_level, tapers)
    return posterior.reshape(LEV, MEMBERS, COLS).transpose(1, 0, 2)


def solution(mesh):
    return jax.shard_map(
        per_device,
        mesh=mesh,
        in_specs=(P(None, "lev", "tile"), P(), P(), P(), P(), P()),
        out_specs=P(None, "lev", "tile"),
        check_vma=False,
    )
```

```python
import jax
import jax.numpy as jnp
from jax import lax
from jax.experimental import pallas as pl
from jax.experimental.pallas import tpu as pltpu
from jax.sharding import PartitionSpec as P

MEMBERS = 80
OBS = 256
NB = 8
COLS = 1024
LEV = 6
COLUMNS = 32768
RADIUS = 2560
VREACH = 12
TILES = 32
NEAR = -(-RADIUS // COLS)

HALF = 80
PIECE = 5
PLANE = 16
DEPTH = 8

F32 = jnp.float32
BF16 = jnp.bfloat16


def down(row):
    return jnp.broadcast_to(row, (128, OBS)).T


def inverse_of(value):
    rough = pl.reciprocal(value, approx=True)
    return rough * (2.0 - value * rough)


def exchange_kernel(ens_h, tile_h, col_h, lev_h, fac_h, *refs):
    (obs_out, ghi_out, glo_out), refs = refs[:3], refs[3:]
    taper_out, refs = refs[:NB - 1], refs[NB - 1:]
    exchange_body((ens_h, tile_h, col_h, lev_h, fac_h), obs_out, ghi_out, glo_out, taper_out, *refs)


def exchange_body(given, obs_out, ghi_out, glo_out, taper_out,
                  ens, tile_r, col_r, lev_r, fac, load, buf, r0, s0, r1, s1, r2, s2, full,
                  send0, recv0, send1, recv1, send2, recv2, send3, recv3, send4, recv4):
    t = lax.axis_index("tile")
    l = lax.axis_index("lev")
    core = t % 2
    z_lo = (t // 2) % 4
    x = t // 8
    y = l // 2
    z_hi = l % 2
    plane = x * 4 + y
    z = z_hi * 4 + z_lo

    def plane_peer(d):
        j = (plane + d) % PLANE
        return j, {"tile": (j // 4) * 8 + z_lo * 2 + core, "lev": (j % 4) * 2 + z_hi}

    def depth_peer(d):
        j = (z + d) % DEPTH
        return j, {"tile": x * 8 + (j % 4) * 2 + core, "lev": y * 2 + j // 4}

    loads = [pltpu.make_async_copy(src, dst, load.at[i])
             for i, (src, dst) in enumerate(zip(given, (ens, tile_r, col_r, lev_r, fac)))]
    for i in (1, 2, 3, 0, 4):
        loads[i].start()

    mate = {"tile": t + 1 - 2 * core, "lev": l}
    peers = [mate] + [plane_peer(d)[1] for d in range(1, PLANE)]
    peers += [depth_peer(d)[1] for d in range(1, DEPTH)]
    barrier = pltpu.get_barrier_semaphore()
    for peer in peers:
        pl.semaphore_signal(barrier, inc=1, device_id=peer, device_id_type=pl.DeviceIdType.MESH)

    for i in range(4):
        loads[i].wait()

    def pick(b, carry):
        owned = tile_r[pl.ds(b, 1), :] == t
        column = jnp.where(owned, col_r[pl.ds(b, 1), :], -1)
        level = lev_r[pl.ds(b, 1), :] - l * LEV
        rows = lax.broadcasted_iota(jnp.int32, (COLS, OBS), 0)
        onehot = jnp.where(rows == column, 1.0, 0.0).astype(BF16)
        got = jnp.dot(ens[...], onehot, preferred_element_type=F32)
        total = jnp.zeros((MEMBERS, OBS), F32)
        for v in range(LEV):
            total = total + jnp.where(level == v, got[v * MEMBERS:(v + 1) * MEMBERS], 0.0)
        for h in range(2):
            for mb in range(10):
                buf[b * 20 + h * 10 + mb] = total[mb * 8:mb * 8 + 8, h * 128:h * 128 + 128]
        return carry

    def pair_copy(j):
        return pltpu.make_async_remote_copy(
            src_ref=buf.at[pl.ds((1 - core) * HALF + j * PIECE, PIECE)],
            dst_ref=r0.at[j], send_sem=send0.at[j], recv_sem=recv0.at[j],
            device_id=mate, device_id_type=pl.DeviceIdType.MESH)

    for step in range(4):
        from_batch = (step * 2 + 4 * (1 - core)) % NB
        lax.fori_loop(0, 2, lambda i, c, from_batch=from_batch: pick(from_batch + i, c), 0, unroll=True)
        if step == 0:
            pl.semaphore_wait(barrier, len(peers))
        if step < 2:
            for j in range(step * 8, step * 8 + 8):
                pair_copy(j).start()

    order = list(range(1, PLANE)) + [0]
    spread_out = {}
    for d in order:
        j, peer = plane_peer(d)
        pair_copy(j).wait_recv()
        s0[j] = buf[pl.ds(core * HALF + j * PIECE, PIECE)] + r0[j]
        if d:
            c = pltpu.make_async_remote_copy(
                src_ref=s0.at[j], dst_ref=r1.at[d], send_sem=send1.at[d], recv_sem=recv1.at[d],
                device_id=peer, device_id_type=pl.DeviceIdType.MESH)
            c.start()
            spread_out[d] = c

    loads[4].wait()

    def gram(b, carry):
        f = fac[b]
        f_t = f.T
        hi, hi_t = f.astype(BF16), f_t.astype(BF16)
        lo, lo_t = (f - hi.astype(F32)).astype(BF16), (f_t - hi_t.astype(F32)).astype(BF16)
        g = (jnp.dot(hi_t, hi, preferred_element_type=F32)
             + (jnp.dot(hi_t, lo, preferred_element_type=F32)
                + jnp.dot(lo_t, hi, preferred_element_type=F32)))
        g_hi = g.astype(BF16)
        ghi_out[b] = g_hi
        glo_out[b] = (g - g_hi.astype(F32)).astype(BF16)
        return carry
    lax.fori_loop(0, NB // 2, gram, 0, unroll=2)

    reach_sq = float(VREACH * VREACH)
    inverse = 1.0 / (MEMBERS - 1)

    def tapers_of(b):
        gcol_d = down((tile_r[b:b + 1, :] * COLS + col_r[b:b + 1, :]).astype(F32))
        level_d = down(lev_r[b:b + 1, :].astype(F32))

        def later(b2, carry):
            g2 = (tile_r[pl.ds(b2, 1), :] * COLS + col_r[pl.ds(b2, 1), :]).astype(F32)
            l2 = lev_r[pl.ds(b2, 1), :].astype(F32)
            for h in range(2):
                cut = slice(h * 128, h * 128 + 128)
                dist = jnp.abs(gcol_d - g2[:, cut])
                dist = jnp.minimum(dist, COLUMNS - dist)
                taper = jnp.maximum(0.0, 1.0 - dist * (1.0 / RADIUS))
                off = level_d - l2[:, cut]
                vert = (reach_sq * inverse) * inverse_of(reach_sq + off * off)
                place = pl.multiple_of((b2 - b - 1) * OBS + h * 128, 128)
                taper_out[b][:, pl.ds(place, 128)] = taper * vert
            return carry
        lax.fori_loop(b + 1, NB, later, 0)

    total = s0[plane]
    for d in range(1, PLANE):
        spread_out[d].wait_recv()
        total = total + r1[d]
    s1[...] = total
    along = {}
    for d in range(1, DEPTH):
        _, peer = depth_peer(d)
        c = pltpu.make_async_remote_copy(
            src_ref=s1, dst_ref=r2.at[d], send_sem=send2.at[d], recv_sem=recv2.at[d],
            device_id=peer, device_id_type=pl.DeviceIdType.MESH)
        c.start()
        along[d] = c
    lax.fori_loop(NB // 2, NB, gram, 0, unroll=2)
    for d in range(1, DEPTH):
        along[d].wait_recv()
        total = total + r2[d]
    s2[...] = total
    full[pl.ds(core * HALF + plane * PIECE, PIECE)] = total

    gathered = {}
    for d in range(1, PLANE):
        _, peer = plane_peer(d)
        c = pltpu.make_async_remote_copy(
            src_ref=s2, dst_ref=full.at[pl.ds(core * HALF + plane * PIECE, PIECE)],
            send_sem=send3.at[d], recv_sem=recv3.at[d],
            device_id=peer, device_id_type=pl.DeviceIdType.MESH)
        c.start()
        gathered[d] = c
    passed = {}
    beside = {1: (0, 1), 5: (2,), 9: (3,), 13: (4, 5, 6)}
    for d in range(PLANE):
        for b in beside.get(d, ()):
            tapers_of(b)
        j = (plane - d + PLANE) % PLANE
        if d:
            gathered[d].wait_recv()
        part = full.at[pl.ds(core * HALF + j * PIECE, PIECE)]
        c = pltpu.make_async_remote_copy(
            src_ref=part, dst_ref=part, send_sem=send4.at[d], recv_sem=recv4.at[d],
            device_id=mate, device_id_type=pl.DeviceIdType.MESH)
        c.start()
        passed[d] = c
    for d in range(PLANE):
        passed[d].wait_recv()

    def unpack(cb, carry):
        for mb in range(10):
            obs_out[mb * 8:mb * 8 + 8, pl.ds(pl.multiple_of(cb * 128, 128), 128)] = full[cb * 10 + mb]
        return carry
    lax.fori_loop(0, 16, unpack, 0)

    for d in range(PLANE):
        pair_copy(d).wait_send()
        passed[d].wait_send()
        if d:
            spread_out[d].wait_send()
            gathered[d].wait_send()
        if 0 < d < DEPTH:
            along[d].wait_send()


def exchange(ensemble, obs_tile, obs_column, obs_level, factor):
    vmem = pl.BlockSpec(memory_space=pltpu.VMEM)
    dma = pltpu.SemaphoreType.DMA
    piece = (PIECE, 8, 128)
    return pl.pallas_call(
        exchange_kernel,
        out_shape=(
            jax.ShapeDtypeStruct((MEMBERS, NB * OBS), F32),
            jax.ShapeDtypeStruct((NB, OBS, OBS), BF16),
            jax.ShapeDtypeStruct((NB, OBS, OBS), BF16),
        ) + tuple(jax.ShapeDtypeStruct((OBS, (NB - 1 - b) * OBS), F32) for b in range(NB - 1)),
        in_specs=[pl.BlockSpec(memory_space=pltpu.HBM)] * 5,
        out_specs=(vmem,) * (NB + 2),
        scratch_shapes=[
            pltpu.VMEM((LEV * MEMBERS, COLS), BF16),
            pltpu.VMEM((NB, OBS), jnp.int32),
            pltpu.VMEM((NB, OBS), jnp.int32),
            pltpu.VMEM((NB, OBS), jnp.int32),
            pltpu.VMEM((NB, OBS, OBS), F32),
            dma((5,)),
            pltpu.VMEM((2 * HALF, 8, 128), F32),
            pltpu.VMEM((PLANE,) + piece, F32),
            pltpu.VMEM((PLANE,) + piece, F32),
            pltpu.VMEM((PLANE,) + piece, F32),
            pltpu.VMEM(piece, F32),
            pltpu.VMEM((DEPTH,) + piece, F32),
            pltpu.VMEM(piece, F32),
            pltpu.VMEM((2 * HALF, 8, 128), F32),
            dma((PLANE,)), dma((PLANE,)), dma((PLANE,)), dma((PLANE,)),
            dma((DEPTH,)), dma((DEPTH,)),
            dma((PLANE,)), dma((PLANE,)), dma((PLANE,)), dma((PLANE,)),
        ],
        compiler_params=pltpu.CompilerParams(
            collective_id=0, has_side_effects=True, vmem_limit_bytes=14 * 1024 * 1024),
        name="exchange",
    )(*(pltpu.with_memory_space_constraint(a, pltpu.HBM)
        for a in (ensemble, obs_tile, obs_column, obs_level, factor)))


def centred(values):
    return values - jnp.sum(values, axis=0, keepdims=True) * (1.0 / MEMBERS)


def update_kernel(x_ref, obs_ref, pert, ghi, glo, tile_r, col_r, lev_r, *refs):
    tapers = refs[:NB - 1]
    out, state, aug, devs, weights, gcols, levels, horiz, counts = refs[NB - 1:]
    t = lax.axis_index("tile")
    first = lax.axis_index("lev") * LEV
    state[...] = x_ref[...].astype(F32)
    aug[...] = obs_ref[...]
    reach_sq = float(VREACH * VREACH)
    inverse = 1.0 / (MEMBERS - 1)

    low = (t + TILES - NEAR) % TILES
    turns = []
    for b in range(NB):
        owner = tile_r[b:b + 1, :]
        rel = owner - low
        rel = jnp.where(rel < 0, rel + TILES, rel)
        counts[b] = jnp.sum(jnp.where(rel < 2 * NEAR + 1, 1.0, 0.0)).astype(jnp.int32)
        skipped = jnp.sum(jnp.where(owner < low, 1.0, 0.0)).astype(jnp.int32)
        turns.append(lax.rem(OBS - skipped, OBS))

    def column_step(b):
        priors = aug[:, b * OBS:(b + 1) * OBS]
        prior_dev = centred(priors)
        innovation = pert[b] - priors
        in_hi = innovation.astype(BF16)
        in_lo = (innovation - in_hi.astype(F32)).astype(BF16)
        g_hi = ghi[b]
        full_weight = (jnp.dot(in_hi, g_hi, preferred_element_type=F32)
                       + jnp.dot(in_lo, g_hi, preferred_element_type=F32)
                       + jnp.dot(in_hi, glo[b], preferred_element_type=F32))
        if b + 1 < NB:
            rest = slice((b + 1) * OBS, NB * OBS)
            values = aug[:, rest]
            covar = jnp.dot(prior_dev.T.astype(BF16), centred(values).astype(BF16),
                            preferred_element_type=F32)
            tapered = (covar * tapers[b][...]).astype(BF16)
            aug[:, rest] = values + jnp.dot(full_weight.astype(BF16), tapered,
                                            preferred_element_type=F32)
        dev_t = pltpu.roll(prior_dev, turns[b], 1).T
        weight = pltpu.roll(full_weight, turns[b], 1).astype(BF16)
        gcol = (tile_r[b:b + 1, :] * COLS + col_r[b:b + 1, :]).astype(F32)
        gcol_d = pltpu.roll(jnp.broadcast_to(gcol, (128, OBS)), turns[b], 1).T
        lev = lev_r[b:b + 1, :].astype(F32)
        level_d = pltpu.roll(jnp.broadcast_to(lev, (128, OBS)), turns[b], 1).T
        return dev_t, weight, gcol_d, level_d

    def regress(slot, width, dev_t, weight, gcol_d, level_d):
        lanes = lax.broadcasted_iota(jnp.int32, (width, 128), 1)
        for q in range(COLS // 128):
            dist = jnp.abs(gcol_d[0:width] - (t * COLS + q * 128 + lanes).astype(F32))
            dist = jnp.minimum(dist, COLUMNS - dist)
            horiz[slot, 0:width, q * 128:q * 128 + 128] = jnp.maximum(0.0, 1.0 - dist * (1.0 / RADIUS))
        weight = weight[:, 0:width]
        level_d = level_d[0:width, 0:MEMBERS]
        dev_t = dev_t[0:width]

        def first_dot(v):
            off = level_d - (first + v).astype(F32)
            vert = (reach_sq * inverse) * inverse_of(reach_sq + off * off)
            values = state[v * MEMBERS:(v + 1) * MEMBERS, :]
            return jnp.dot((dev_t * vert).astype(BF16), centred(values).astype(BF16),
                           preferred_element_type=F32)

        ahead = first_dot(0)
        for v in range(LEV):
            covar = ahead
            if v + 1 < LEV:
                ahead = first_dot(v + 1)
            rows = slice(v * MEMBERS, (v + 1) * MEMBERS)
            tapered = (covar * horiz[slot, 0:width, :]).astype(BF16)
            state[rows, :] = state[rows, :] + jnp.dot(weight, tapered, preferred_element_type=F32)

    most = counts[0]
    for b in range(1, NB):
        most = jnp.maximum(most, counts[b])

    def straight(width):
        for b in range(NB):
            regress(b % 2, width, *column_step(b))
        out[...] = state[...].astype(BF16)

    for low_width, width in ((-1, 128), (128, 160)):
        @pl.when((most > low_width) & (most <= width))
        def _(width=width):
            straight(width)

    @pl.when(most > 160)
    def _():
        for b in range(NB):
            devs[b], weights[b], gcols[b], levels[b] = column_step(b)

        def batch(b, carry):
            regress(0, OBS, devs[b], weights[b], gcols[b], levels[b])
            return carry
        lax.fori_loop(0, NB, batch, 0)
        out[...] = state[...].astype(BF16)


def update(x, obs, perturbed, ghi, glo, obs_tile, obs_column, obs_level, tapers):
    vmem = pl.BlockSpec(memory_space=pltpu.VMEM)
    return pl.pallas_call(
        update_kernel,
        out_shape=jax.ShapeDtypeStruct((LEV * MEMBERS, COLS), BF16),
        in_specs=[vmem] * (8 + NB - 1),
        out_specs=vmem,
        scratch_shapes=[
            pltpu.VMEM((LEV * MEMBERS, COLS), F32),
            pltpu.VMEM((MEMBERS, NB * OBS), F32),
            pltpu.VMEM((NB, OBS, MEMBERS), F32),
            pltpu.VMEM((NB, MEMBERS, OBS), BF16),
            pltpu.VMEM((NB, OBS, 128), F32),
            pltpu.VMEM((NB, OBS, 128), F32),
            pltpu.VMEM((2, OBS, COLS), F32),
            pltpu.SMEM((NB,), jnp.int32),
        ],
        compiler_params=pltpu.CompilerParams(vmem_limit_bytes=28 * 1024 * 1024),
        name="update",
    )(x, obs, perturbed, ghi, glo, obs_tile, obs_column, obs_level, *tapers)


def per_device(ensemble, perturbed, factor, obs_tile, obs_column, obs_level):
    x = ensemble.transpose(1, 0, 2).reshape(LEV * MEMBERS, COLS)
    obs, ghi, glo, *tapers = exchange(x, obs_tile, obs_column, obs_level, factor)
    posterior = update(x, obs, perturbed, ghi, glo, obs_tile, obs_column, obs_level, tapers)
    return posterior.reshape(LEV, MEMBERS, COLS).transpose(1, 0, 2)


def solution(mesh):
    return jax.shard_map(
        per_device,
        mesh=mesh,
        in_specs=(P(None, "lev", "tile"), P(), P(), P(), P(), P()),
        out_specs=P(None, "lev", "tile"),
        check_vma=False,
    )
```

```python
import jax
import jax.numpy as jnp
from jax import lax
from jax.experimental import pallas as pl
from jax.experimental.pallas import tpu as pltpu
from jax.sharding import PartitionSpec as P

MEMBERS = 80
OBS = 256
NB = 8
COLS = 1024
LEV = 6
COLUMNS = 32768
RADIUS = 2560
VREACH = 12
TILES = 32
NEAR = -(-RADIUS // COLS)

HALF = 80
PIECE = 5
PLANE = 16
PARTS = ((0, 3), (3, 2))
DEPTH = 8

F32 = jnp.float32
BF16 = jnp.bfloat16


def down(row):
    return jnp.broadcast_to(row, (128, OBS)).T


def inverse_of(value):
    rough = pl.reciprocal(value, approx=True)
    return rough * (2.0 - value * rough)


def exchange_kernel(ens_h, tile_h, col_h, lev_h, fac_h, *refs):
    (obs_out, ghi_out, glo_out), refs = refs[:3], refs[3:]
    taper_out, refs = refs[:NB - 1], refs[NB - 1:]
    exchange_body((ens_h, tile_h, col_h, lev_h, fac_h), obs_out, ghi_out, glo_out, taper_out, *refs)


def exchange_body(given, obs_out, ghi_out, glo_out, taper_out,
                  ens, tile_r, col_r, lev_r, fac, load, buf, r0, s0, r1, s1, r2, s2, full,
                  send0, recv0, send1, recv1, send2, recv2, send3, recv3, send4, recv4):
    t = lax.axis_index("tile")
    l = lax.axis_index("lev")
    core = t % 2
    z_lo = (t // 2) % 4
    x = t // 8
    y = l // 2
    z_hi = l % 2
    plane = x * 4 + y
    z = z_hi * 4 + z_lo

    def plane_peer(d):
        j = (plane + d) % PLANE
        return j, {"tile": (j // 4) * 8 + z_lo * 2 + core, "lev": (j % 4) * 2 + z_hi}

    def depth_peer(d):
        j = (z + d) % DEPTH
        return j, {"tile": x * 8 + (j % 4) * 2 + core, "lev": y * 2 + j // 4}

    loads = [pltpu.make_async_copy(src, dst, load.at[i])
             for i, (src, dst) in enumerate(zip(given, (ens, tile_r, col_r, lev_r, fac)))]
    for i in (1, 2, 3, 0, 4):
        loads[i].start()

    mate = {"tile": t + 1 - 2 * core, "lev": l}
    peers = [mate] + [plane_peer(d)[1] for d in range(1, PLANE)]
    peers += [depth_peer(d)[1] for d in range(1, DEPTH)]
    barrier = pltpu.get_barrier_semaphore()
    for peer in peers:
        pl.semaphore_signal(barrier, inc=1, device_id=peer, device_id_type=pl.DeviceIdType.MESH)

    for i in range(4):
        loads[i].wait()

    def pick(b, carry):
        owned = tile_r[pl.ds(b, 1), :] == t
        column = jnp.where(owned, col_r[pl.ds(b, 1), :], -1)
        level = lev_r[pl.ds(b, 1), :] - l * LEV
        rows = lax.broadcasted_iota(jnp.int32, (COLS, OBS), 0)
        onehot = jnp.where(rows == column, 1.0, 0.0).astype(BF16)
        got = jnp.dot(ens[...], onehot, preferred_element_type=F32)
        total = jnp.zeros((MEMBERS, OBS), F32)
        for v in range(LEV):
            total = total + jnp.where(level == v, got[v * MEMBERS:(v + 1) * MEMBERS], 0.0)
        for h in range(2):
            for mb in range(10):
                buf[b * 20 + h * 10 + mb] = total[mb * 8:mb * 8 + 8, h * 128:h * 128 + 128]
        return carry

    def pair_copy(j):
        return pltpu.make_async_remote_copy(
            src_ref=buf.at[pl.ds((1 - core) * HALF + j * PIECE, PIECE)],
            dst_ref=r0.at[j], send_sem=send0.at[j], recv_sem=recv0.at[j],
            device_id=mate, device_id_type=pl.DeviceIdType.MESH)

    for step in range(4):
        from_batch = (step * 2 + 4 * (1 - core)) % NB
        lax.fori_loop(0, 2, lambda i, c, from_batch=from_batch: pick(from_batch + i, c), 0, unroll=True)
        if step == 0:
            pl.semaphore_wait(barrier, len(peers))
        if step < 2:
            for j in range(step * 8, step * 8 + 8):
                pair_copy(j).start()

    order = list(range(1, PLANE)) + [0]
    def remote(src, dst, send, recv, peer):
        c = pltpu.make_async_remote_copy(
            src_ref=src, dst_ref=dst, send_sem=send, recv_sem=recv,
            device_id=peer, device_id_type=pl.DeviceIdType.MESH)
        c.start()
        return c

    spread_out, along, gathered, passed = {}, {}, {}, {}
    for p, (at, size) in enumerate(PARTS):
        for d in order:
            j, peer = plane_peer(d)
            if p == 0:
                pair_copy(j).wait_recv()
                s0[j] = buf[pl.ds(core * HALF + j * PIECE, PIECE)] + r0[j]
            if d:
                spread_out[p, d] = remote(s0.at[j, pl.ds(at, size)], r1.at[d, pl.ds(at, size)],
                                          send1.at[p, d], recv1.at[p, d], peer)

    def plane_sum(p):
        at, size = PARTS[p]
        total = s0[plane, at:at + size]
        for d in range(1, PLANE):
            spread_out[p, d].wait_recv()
            total = total + r1[d, at:at + size]
        s1[at:at + size] = total
        for d in range(1, DEPTH):
            along[p, d] = remote(s1.at[pl.ds(at, size)], r2.at[d, pl.ds(at, size)],
                                 send2.at[p, d], recv2.at[p, d], depth_peer(d)[1])

    def depth_sum(p):
        at, size = PARTS[p]
        total = s1[at:at + size]
        for d in range(1, DEPTH):
            along[p, d].wait_recv()
            total = total + r2[d, at:at + size]
        s2[at:at + size] = total
        place = pl.ds(core * HALF + plane * PIECE + at, size)
        full[place] = total
        for d in range(1, PLANE):
            gathered[p, d] = remote(s2.at[pl.ds(at, size)], full.at[place],
                                    send3.at[p, d], recv3.at[p, d], plane_peer(d)[1])

    def forward(p):
        at, size = PARTS[p]
        for d in range(PLANE):
            j = (plane - d + PLANE) % PLANE
            if d:
                gathered[p, d].wait_recv()
            part = full.at[pl.ds(core * HALF + j * PIECE + at, size)]
            passed[p, d] = remote(part, part, send4.at[p, d], recv4.at[p, d], mate)

    loads[4].wait()

    def gram(b, carry):
        f = fac[b]
        f_t = f.T
        hi, hi_t = f.astype(BF16), f_t.astype(BF16)
        lo, lo_t = (f - hi.astype(F32)).astype(BF16), (f_t - hi_t.astype(F32)).astype(BF16)
        g = (jnp.dot(hi_t, hi, preferred_element_type=F32)
             + (jnp.dot(hi_t, lo, preferred_element_type=F32)
                + jnp.dot(lo_t, hi, preferred_element_type=F32)))
        g_hi = g.astype(BF16)
        ghi_out[b] = g_hi
        glo_out[b] = (g - g_hi.astype(F32)).astype(BF16)
        return carry
    reach_sq = float(VREACH * VREACH)
    inverse = 1.0 / (MEMBERS - 1)

    def tapers_of(b):
        gcol_d = down((tile_r[b:b + 1, :] * COLS + col_r[b:b + 1, :]).astype(F32))
        level_d = down(lev_r[b:b + 1, :].astype(F32))

        def later(b2, carry):
            g2 = (tile_r[pl.ds(b2, 1), :] * COLS + col_r[pl.ds(b2, 1), :]).astype(F32)
            l2 = lev_r[pl.ds(b2, 1), :].astype(F32)
            for h in range(2):
                cut = slice(h * 128, h * 128 + 128)
                dist = jnp.abs(gcol_d - g2[:, cut])
                dist = jnp.minimum(dist, COLUMNS - dist)
                taper = jnp.maximum(0.0, 1.0 - dist * (1.0 / RADIUS))
                off = level_d - l2[:, cut]
                vert = (reach_sq * inverse) * inverse_of(reach_sq + off * off)
                place = pl.multiple_of((b2 - b - 1) * OBS + h * 128, 128)
                taper_out[b][:, pl.ds(place, 128)] = taper * vert
            return carry
        lax.fori_loop(b + 1, NB, later, 0)

    lax.fori_loop(0, NB, gram, 0, unroll=2)
    plane_sum(0)
    tapers_of(0)
    plane_sum(1)
    tapers_of(1)
    tapers_of(2)
    depth_sum(0)
    tapers_of(3)
    depth_sum(1)
    for b in range(4, NB - 1):
        tapers_of(b)
    for p in range(2):
        forward(p)
    for p in range(2):
        for d in range(PLANE):
            passed[p, d].wait_recv()

    def unpack(cb, carry):
        for mb in range(10):
            obs_out[mb * 8:mb * 8 + 8, pl.ds(pl.multiple_of(cb * 128, 128), 128)] = full[cb * 10 + mb]
        return carry
    lax.fori_loop(0, 16, unpack, 0)

    for d in range(PLANE):
        pair_copy(d).wait_send()
    for sent in (spread_out, along, gathered, passed):
        for c in sent.values():
            c.wait_send()


def exchange(ensemble, obs_tile, obs_column, obs_level, factor):
    vmem = pl.BlockSpec(memory_space=pltpu.VMEM)
    dma = pltpu.SemaphoreType.DMA
    piece = (PIECE, 8, 128)
    return pl.pallas_call(
        exchange_kernel,
        out_shape=(
            jax.ShapeDtypeStruct((MEMBERS, NB * OBS), F32),
            jax.ShapeDtypeStruct((NB, OBS, OBS), BF16),
            jax.ShapeDtypeStruct((NB, OBS, OBS), BF16),
        ) + tuple(jax.ShapeDtypeStruct((OBS, (NB - 1 - b) * OBS), F32) for b in range(NB - 1)),
        in_specs=[pl.BlockSpec(memory_space=pltpu.HBM)] * 5,
        out_specs=(vmem,) * (NB + 2),
        scratch_shapes=[
            pltpu.VMEM((LEV * MEMBERS, COLS), BF16),
            pltpu.VMEM((NB, OBS), jnp.int32),
            pltpu.VMEM((NB, OBS), jnp.int32),
            pltpu.VMEM((NB, OBS), jnp.int32),
            pltpu.VMEM((NB, OBS, OBS), F32),
            dma((5,)),
            pltpu.VMEM((2 * HALF, 8, 128), F32),
            pltpu.VMEM((PLANE,) + piece, F32),
            pltpu.VMEM((PLANE,) + piece, F32),
            pltpu.VMEM((PLANE,) + piece, F32),
            pltpu.VMEM(piece, F32),
            pltpu.VMEM((DEPTH,) + piece, F32),
            pltpu.VMEM(piece, F32),
            pltpu.VMEM((2 * HALF, 8, 128), F32),
            dma((PLANE,)), dma((PLANE,)), dma((2, PLANE)), dma((2, PLANE)),
            dma((2, DEPTH)), dma((2, DEPTH)),
            dma((2, PLANE)), dma((2, PLANE)), dma((2, PLANE)), dma((2, PLANE)),
        ],
        compiler_params=pltpu.CompilerParams(
            collective_id=0, has_side_effects=True, vmem_limit_bytes=14 * 1024 * 1024),
        name="exchange",
    )(*(pltpu.with_memory_space_constraint(a, pltpu.HBM)
        for a in (ensemble, obs_tile, obs_column, obs_level, factor)))


def centred(values):
    return values - jnp.sum(values, axis=0, keepdims=True) * (1.0 / MEMBERS)


def update_kernel(x_ref, obs_ref, pert, ghi, glo, tile_r, col_r, lev_r, *refs):
    tapers = refs[:NB - 1]
    out, state, aug, devs, weights, gcols, levels, horiz, counts = refs[NB - 1:]
    t = lax.axis_index("tile")
    first = lax.axis_index("lev") * LEV
    state[...] = x_ref[...].astype(F32)
    aug[...] = obs_ref[...]
    reach_sq = float(VREACH * VREACH)
    inverse = 1.0 / (MEMBERS - 1)

    low = (t + TILES - NEAR) % TILES
    turns = []
    for b in range(NB):
        owner = tile_r[b:b + 1, :]
        rel = owner - low
        rel = jnp.where(rel < 0, rel + TILES, rel)
        counts[b] = jnp.sum(jnp.where(rel < 2 * NEAR + 1, 1.0, 0.0)).astype(jnp.int32)
        skipped = jnp.sum(jnp.where(owner < low, 1.0, 0.0)).astype(jnp.int32)
        turns.append(lax.rem(OBS - skipped, OBS))

    def column_step(b):
        priors = aug[:, b * OBS:(b + 1) * OBS]
        prior_dev = centred(priors)
        innovation = pert[b] - priors
        in_hi = innovation.astype(BF16)
        in_lo = (innovation - in_hi.astype(F32)).astype(BF16)
        g_hi = ghi[b]
        full_weight = (jnp.dot(in_hi, g_hi, preferred_element_type=F32)
                       + jnp.dot(in_lo, g_hi, preferred_element_type=F32)
                       + jnp.dot(in_hi, glo[b], preferred_element_type=F32))
        if b + 1 < NB:
            rest = slice((b + 1) * OBS, NB * OBS)
            values = aug[:, rest]
            covar = jnp.dot(prior_dev.T.astype(BF16), centred(values).astype(BF16),
                            preferred_element_type=F32)
            tapered = (covar * tapers[b][...]).astype(BF16)
            aug[:, rest] = values + jnp.dot(full_weight.astype(BF16), tapered,
                                            preferred_element_type=F32)
        dev_t = pltpu.roll(prior_dev, turns[b], 1).T
        weight = pltpu.roll(full_weight, turns[b], 1).astype(BF16)
        gcol = (tile_r[b:b + 1, :] * COLS + col_r[b:b + 1, :]).astype(F32)
        gcol_d = pltpu.roll(jnp.broadcast_to(gcol, (128, OBS)), turns[b], 1).T
        lev = lev_r[b:b + 1, :].astype(F32)
        level_d = pltpu.roll(jnp.broadcast_to(lev, (128, OBS)), turns[b], 1).T
        return dev_t, weight, gcol_d, level_d

    def regress(slot, width, dev_t, weight, gcol_d, level_d):
        lanes = lax.broadcasted_iota(jnp.int32, (width, 128), 1)
        for q in range(COLS // 128):
            dist = jnp.abs(gcol_d[0:width] - (t * COLS + q * 128 + lanes).astype(F32))
            dist = jnp.minimum(dist, COLUMNS - dist)
            horiz[slot, 0:width, q * 128:q * 128 + 128] = jnp.maximum(0.0, 1.0 - dist * (1.0 / RADIUS))
        weight = weight[:, 0:width]
        level_d = level_d[0:width, 0:MEMBERS]
        dev_t = dev_t[0:width]

        def first_dot(v):
            off = level_d - (first + v).astype(F32)
            vert = (reach_sq * inverse) * inverse_of(reach_sq + off * off)
            values = state[v * MEMBERS:(v + 1) * MEMBERS, :]
            return jnp.dot((dev_t * vert).astype(BF16), centred(values).astype(BF16),
                           preferred_element_type=F32)

        ahead = first_dot(0)
        for v in range(LEV):
            covar = ahead
            if v + 1 < LEV:
                ahead = first_dot(v + 1)
            rows = slice(v * MEMBERS, (v + 1) * MEMBERS)
            tapered = (covar * horiz[slot, 0:width, :]).astype(BF16)
            state[rows, :] = state[rows, :] + jnp.dot(weight, tapered, preferred_element_type=F32)

    most = counts[0]
    for b in range(1, NB):
        most = jnp.maximum(most, counts[b])

    def straight(width):
        for b in range(NB):
            regress(b % 2, width, *column_step(b))
        out[...] = state[...].astype(BF16)

    for low_width, width in ((-1, 128), (128, 160)):
        @pl.when((most > low_width) & (most <= width))
        def _(width=width):
            straight(width)

    @pl.when(most > 160)
    def _():
        for b in range(NB):
            devs[b], weights[b], gcols[b], levels[b] = column_step(b)

        def batch(b, carry):
            regress(0, OBS, devs[b], weights[b], gcols[b], levels[b])
            return carry
        lax.fori_loop(0, NB, batch, 0)
        out[...] = state[...].astype(BF16)


def update(x, obs, perturbed, ghi, glo, obs_tile, obs_column, obs_level, tapers):
    vmem = pl.BlockSpec(memory_space=pltpu.VMEM)
    return pl.pallas_call(
        update_kernel,
        out_shape=jax.ShapeDtypeStruct((LEV * MEMBERS, COLS), BF16),
        in_specs=[vmem] * (8 + NB - 1),
        out_specs=vmem,
        scratch_shapes=[
            pltpu.VMEM((LEV * MEMBERS, COLS), F32),
            pltpu.VMEM((MEMBERS, NB * OBS), F32),
            pltpu.VMEM((NB, OBS, MEMBERS), F32),
            pltpu.VMEM((NB, MEMBERS, OBS), BF16),
            pltpu.VMEM((NB, OBS, 128), F32),
            pltpu.VMEM((NB, OBS, 128), F32),
            pltpu.VMEM((2, OBS, COLS), F32),
            pltpu.SMEM((NB,), jnp.int32),
        ],
        compiler_params=pltpu.CompilerParams(vmem_limit_bytes=28 * 1024 * 1024),
        name="update",
    )(x, obs, perturbed, ghi, glo, obs_tile, obs_column, obs_level, *tapers)


def per_device(ensemble, perturbed, factor, obs_tile, obs_column, obs_level):
    x = ensemble.transpose(1, 0, 2).reshape(LEV * MEMBERS, COLS)
    obs, ghi, glo, *tapers = exchange(x, obs_tile, obs_column, obs_level, factor)
    posterior = update(x, obs, perturbed, ghi, glo, obs_tile, obs_column, obs_level, tapers)
    return posterior.reshape(LEV, MEMBERS, COLS).transpose(1, 0, 2)


def solution(mesh):
    return jax.shard_map(
        per_device,
        mesh=mesh,
        in_specs=(P(None, "lev", "tile"), P(), P(), P(), P(), P()),
        out_specs=P(None, "lev", "tile"),
        check_vma=False,
    )
```

```python
import jax
import jax.numpy as jnp
from jax import lax
from jax.experimental import pallas as pl
from jax.experimental.pallas import tpu as pltpu
from jax.sharding import PartitionSpec as P

MEMBERS = 80
OBS = 256
NB = 8
COLS = 1024
LEV = 6
COLUMNS = 32768
RADIUS = 2560
VREACH = 12
TILES = 32
NEAR = -(-RADIUS // COLS)

HALF = 80
PIECE = 5
PLANE = 16
PARTS = ((0, 3), (3, 2))
DEPTH = 8

F32 = jnp.float32
BF16 = jnp.bfloat16


def down(row):
    return jnp.broadcast_to(row, (128, OBS)).T


def inverse_of(value):
    rough = pl.reciprocal(value, approx=True)
    return rough * (2.0 - value * rough)


def exchange_kernel(ens_h, tile_h, col_h, lev_h, fac_h, *refs):
    (obs_out, ghi_out, glo_out), refs = refs[:3], refs[3:]
    taper_out, refs = refs[:NB - 1], refs[NB - 1:]
    exchange_body((ens_h, tile_h, col_h, lev_h, fac_h), obs_out, ghi_out, glo_out, taper_out, *refs)


def exchange_body(given, obs_out, ghi_out, glo_out, taper_out,
                  ens, tile_r, col_r, lev_r, fac, load, buf, r0, s0, r1, s1, r2, s2, full,
                  send0, recv0, send1, recv1, send2, recv2, send3, recv3, send4, recv4):
    t = lax.axis_index("tile")
    l = lax.axis_index("lev")
    core = t % 2
    z_lo = (t // 2) % 4
    x = t // 8
    y = l // 2
    z_hi = l % 2
    plane = x * 4 + y
    z = z_hi * 4 + z_lo

    def plane_peer(d):
        j = (plane + d) % PLANE
        return j, {"tile": (j // 4) * 8 + z_lo * 2 + core, "lev": (j % 4) * 2 + z_hi}

    def depth_peer(d):
        j = (z + d) % DEPTH
        return j, {"tile": x * 8 + (j % 4) * 2 + core, "lev": y * 2 + j // 4}

    loads = [pltpu.make_async_copy(src, dst, load.at[i])
             for i, (src, dst) in enumerate(zip(given, (ens, tile_r, col_r, lev_r, fac)))]
    for i in (1, 2, 3, 0, 4):
        loads[i].start()

    mate = {"tile": t + 1 - 2 * core, "lev": l}
    peers = [mate] + [plane_peer(d)[1] for d in range(1, PLANE)]
    peers += [depth_peer(d)[1] for d in range(1, DEPTH)]
    barrier = pltpu.get_barrier_semaphore()
    for peer in peers:
        pl.semaphore_signal(barrier, inc=1, device_id=peer, device_id_type=pl.DeviceIdType.MESH)

    for i in range(4):
        loads[i].wait()

    def pick(b, carry):
        owned = tile_r[pl.ds(b, 1), :] == t
        column = jnp.where(owned, col_r[pl.ds(b, 1), :], -1)
        level = lev_r[pl.ds(b, 1), :] - l * LEV
        rows = lax.broadcasted_iota(jnp.int32, (COLS, OBS), 0)
        onehot = jnp.where(rows == column, 1.0, 0.0).astype(BF16)
        got = jnp.dot(ens[...], onehot, preferred_element_type=F32)
        total = jnp.zeros((MEMBERS, OBS), F32)
        for v in range(LEV):
            total = total + jnp.where(level == v, got[v * MEMBERS:(v + 1) * MEMBERS], 0.0)
        for h in range(2):
            for mb in range(10):
                buf[b * 20 + h * 10 + mb] = total[mb * 8:mb * 8 + 8, h * 128:h * 128 + 128]
        return carry

    def pair_copy(step):
        return pltpu.make_async_remote_copy(
            src_ref=buf.at[pl.ds((1 - core) * HALF + step * 8 * PIECE, 8 * PIECE)],
            dst_ref=r0.at[pl.ds(step * 8 * PIECE, 8 * PIECE)],
            send_sem=send0.at[step], recv_sem=recv0.at[step],
            device_id=mate, device_id_type=pl.DeviceIdType.MESH)

    for step in range(4):
        from_batch = (step * 2 + 4 * (1 - core)) % NB
        lax.fori_loop(0, 2, lambda i, c, from_batch=from_batch: pick(from_batch + i, c), 0, unroll=True)
        if step == 0:
            pl.semaphore_wait(barrier, len(peers))
        if step < 2:
            pair_copy(step).start()

    order = list(range(1, PLANE)) + [0]
    def remote(src, dst, send, recv, peer):
        c = pltpu.make_async_remote_copy(
            src_ref=src, dst_ref=dst, send_sem=send, recv_sem=recv,
            device_id=peer, device_id_type=pl.DeviceIdType.MESH)
        c.start()
        return c

    spread_out, along, gathered, passed = {}, {}, {}, {}
    for step in range(2):
        pair_copy(step).wait_recv()
    for p, (at, size) in enumerate(PARTS):
        for d in order:
            j, peer = plane_peer(d)
            if p == 0:
                s0[j] = buf[pl.ds(core * HALF + j * PIECE, PIECE)] + r0[pl.ds(j * PIECE, PIECE)]
            if d:
                spread_out[p, d] = remote(s0.at[j, pl.ds(at, size)], r1.at[d, pl.ds(at, size)],
                                          send1.at[p, d], recv1.at[p, d], peer)

    def plane_sum(p):
        at, size = PARTS[p]
        total = s0[plane, at:at + size]
        for d in range(1, PLANE):
            spread_out[p, d].wait_recv()
            total = total + r1[d, at:at + size]
        s1[at:at + size] = total
        for d in range(1, DEPTH):
            along[p, d] = remote(s1.at[pl.ds(at, size)], r2.at[d, pl.ds(at, size)],
                                 send2.at[p, d], recv2.at[p, d], depth_peer(d)[1])

    def depth_sum(p):
        at, size = PARTS[p]
        total = s1[at:at + size]
        for d in range(1, DEPTH):
            along[p, d].wait_recv()
            total = total + r2[d, at:at + size]
        s2[at:at + size] = total
        place = pl.ds(core * HALF + plane * PIECE + at, size)
        full[place] = total
        for d in range(1, PLANE):
            gathered[p, d] = remote(s2.at[pl.ds(at, size)], full.at[place],
                                    send3.at[p, d], recv3.at[p, d], plane_peer(d)[1])

    loads[4].wait()

    def gram(b, carry):
        f = fac[b]
        f_t = f.T
        hi, hi_t = f.astype(BF16), f_t.astype(BF16)
        lo, lo_t = (f - hi.astype(F32)).astype(BF16), (f_t - hi_t.astype(F32)).astype(BF16)
        g = (jnp.dot(hi_t, hi, preferred_element_type=F32)
             + (jnp.dot(hi_t, lo, preferred_element_type=F32)
                + jnp.dot(lo_t, hi, preferred_element_type=F32)))
        g_hi = g.astype(BF16)
        ghi_out[b] = g_hi
        glo_out[b] = (g - g_hi.astype(F32)).astype(BF16)
        return carry
    reach_sq = float(VREACH * VREACH)
    inverse = 1.0 / (MEMBERS - 1)

    def tapers_of(b):
        gcol_d = down((tile_r[b:b + 1, :] * COLS + col_r[b:b + 1, :]).astype(F32))
        level_d = down(lev_r[b:b + 1, :].astype(F32))

        def later(b2, carry):
            g2 = (tile_r[pl.ds(b2, 1), :] * COLS + col_r[pl.ds(b2, 1), :]).astype(F32)
            l2 = lev_r[pl.ds(b2, 1), :].astype(F32)
            for h in range(2):
                cut = slice(h * 128, h * 128 + 128)
                dist = jnp.abs(gcol_d - g2[:, cut])
                dist = jnp.minimum(dist, COLUMNS - dist)
                taper = jnp.maximum(0.0, 1.0 - dist * (1.0 / RADIUS))
                off = level_d - l2[:, cut]
                vert = (reach_sq * inverse) * inverse_of(reach_sq + off * off)
                place = pl.multiple_of((b2 - b - 1) * OBS + h * 128, 128)
                taper_out[b][:, pl.ds(place, 128)] = taper * vert
            return carry
        lax.fori_loop(b + 1, NB, later, 0)

    lax.fori_loop(0, NB, gram, 0, unroll=2)
    plane_sum(0)
    tapers_of(0)
    plane_sum(1)
    tapers_of(1)
    tapers_of(2)
    depth_sum(0)
    tapers_of(3)
    depth_sum(1)
    for b in range(4, NB - 1):
        tapers_of(b)
    for step in range(2):
        pair_copy(step).wait_send()
    for sent in (spread_out, along):
        for c in sent.values():
            c.wait_send()
    for d in range(PLANE):
        j = (plane - d + PLANE) % PLANE
        if d:
            for p in range(2):
                gathered[p, d].wait_recv()
        part = full.at[pl.ds(core * HALF + j * PIECE, PIECE)]
        passed[d] = remote(part, part, send4.at[d], recv4.at[d], mate)

    def unpack(cb, carry):
        for mb in range(10):
            obs_out[mb * 8:mb * 8 + 8, pl.ds(pl.multiple_of(cb * 128, 128), 128)] = full[cb * 10 + mb]
        return carry
    lax.fori_loop(core * 8, core * 8 + 8, unpack, 0)
    for c in gathered.values():
        c.wait_send()
    for d in range(PLANE):
        passed[d].wait_recv()
    lax.fori_loop(8 - core * 8, 16 - core * 8, unpack, 0)
    for d in range(PLANE):
        passed[d].wait_send()


def exchange(ensemble, obs_tile, obs_column, obs_level, factor):
    vmem = pl.BlockSpec(memory_space=pltpu.VMEM)
    dma = pltpu.SemaphoreType.DMA
    piece = (PIECE, 8, 128)
    return pl.pallas_call(
        exchange_kernel,
        out_shape=(
            jax.ShapeDtypeStruct((MEMBERS, NB * OBS), F32),
            jax.ShapeDtypeStruct((NB, OBS, OBS), BF16),
            jax.ShapeDtypeStruct((NB, OBS, OBS), BF16),
        ) + tuple(jax.ShapeDtypeStruct((OBS, (NB - 1 - b) * OBS), F32) for b in range(NB - 1)),
        in_specs=[pl.BlockSpec(memory_space=pltpu.HBM)] * 5,
        out_specs=(vmem,) * (NB + 2),
        scratch_shapes=[
            pltpu.VMEM((LEV * MEMBERS, COLS), BF16),
            pltpu.VMEM((NB, OBS), jnp.int32),
            pltpu.VMEM((NB, OBS), jnp.int32),
            pltpu.VMEM((NB, OBS), jnp.int32),
            pltpu.VMEM((NB, OBS, OBS), F32),
            dma((5,)),
            pltpu.VMEM((2 * HALF, 8, 128), F32),
            pltpu.VMEM((HALF, 8, 128), F32),
            pltpu.VMEM((PLANE,) + piece, F32),
            pltpu.VMEM((PLANE,) + piece, F32),
            pltpu.VMEM(piece, F32),
            pltpu.VMEM((DEPTH,) + piece, F32),
            pltpu.VMEM(piece, F32),
            pltpu.VMEM((2 * HALF, 8, 128), F32),
            dma((2,)), dma((2,)), dma((2, PLANE)), dma((2, PLANE)),
            dma((2, DEPTH)), dma((2, DEPTH)),
            dma((2, PLANE)), dma((2, PLANE)), dma((PLANE,)), dma((PLANE,)),
        ],
        compiler_params=pltpu.CompilerParams(
            collective_id=0, has_side_effects=True, vmem_limit_bytes=14 * 1024 * 1024),
        name="exchange",
    )(*(pltpu.with_memory_space_constraint(a, pltpu.HBM)
        for a in (ensemble, obs_tile, obs_column, obs_level, factor)))


def centred(values):
    return values - jnp.sum(values, axis=0, keepdims=True) * (1.0 / MEMBERS)


def update_kernel(x_ref, obs_ref, pert, ghi, glo, tile_r, col_r, lev_r, *refs):
    tapers = refs[:NB - 1]
    out, state, aug, devs, weights, gcols, levels, horiz, counts = refs[NB - 1:]
    t = lax.axis_index("tile")
    first = lax.axis_index("lev") * LEV
    state[...] = x_ref[...].astype(F32)
    aug[...] = obs_ref[...]
    reach_sq = float(VREACH * VREACH)
    inverse = 1.0 / (MEMBERS - 1)

    low = (t + TILES - NEAR) % TILES
    turns = []
    for b in range(NB):
        owner = tile_r[b:b + 1, :]
        rel = owner - low
        rel = jnp.where(rel < 0, rel + TILES, rel)
        counts[b] = jnp.sum(jnp.where(rel < 2 * NEAR + 1, 1.0, 0.0)).astype(jnp.int32)
        skipped = jnp.sum(jnp.where(owner < low, 1.0, 0.0)).astype(jnp.int32)
        turns.append(lax.rem(OBS - skipped, OBS))

    def column_step(b):
        priors = aug[:, b * OBS:(b + 1) * OBS]
        prior_dev = centred(priors)
        innovation = pert[b] - priors
        in_hi = innovation.astype(BF16)
        in_lo = (innovation - in_hi.astype(F32)).astype(BF16)
        g_hi = ghi[b]
        full_weight = (jnp.dot(in_hi, g_hi, preferred_element_type=F32)
                       + jnp.dot(in_lo, g_hi, preferred_element_type=F32)
                       + jnp.dot(in_hi, glo[b], preferred_element_type=F32))
        if b + 1 < NB:
            rest = slice((b + 1) * OBS, NB * OBS)
            values = aug[:, rest]
            covar = jnp.dot(prior_dev.T.astype(BF16), centred(values).astype(BF16),
                            preferred_element_type=F32)
            tapered = (covar * tapers[b][...]).astype(BF16)
            aug[:, rest] = values + jnp.dot(full_weight.astype(BF16), tapered,
                                            preferred_element_type=F32)
        dev_t = pltpu.roll(prior_dev, turns[b], 1).T
        weight = pltpu.roll(full_weight, turns[b], 1).astype(BF16)
        gcol = (tile_r[b:b + 1, :] * COLS + col_r[b:b + 1, :]).astype(F32)
        gcol_d = pltpu.roll(jnp.broadcast_to(gcol, (128, OBS)), turns[b], 1).T
        lev = lev_r[b:b + 1, :].astype(F32)
        level_d = pltpu.roll(jnp.broadcast_to(lev, (128, OBS)), turns[b], 1).T
        return dev_t, weight, gcol_d, level_d

    def regress(slot, width, dev_t, weight, gcol_d, level_d):
        lanes = lax.broadcasted_iota(jnp.int32, (width, 128), 1)
        for q in range(COLS // 128):
            dist = jnp.abs(gcol_d[0:width] - (t * COLS + q * 128 + lanes).astype(F32))
            dist = jnp.minimum(dist, COLUMNS - dist)
            horiz[slot, 0:width, q * 128:q * 128 + 128] = jnp.maximum(0.0, 1.0 - dist * (1.0 / RADIUS))
        weight = weight[:, 0:width]
        level_d = level_d[0:width, 0:MEMBERS]
        dev_t = dev_t[0:width]

        def first_dot(v):
            off = level_d - (first + v).astype(F32)
            vert = (reach_sq * inverse) * inverse_of(reach_sq + off * off)
            values = state[v * MEMBERS:(v + 1) * MEMBERS, :]
            return jnp.dot((dev_t * vert).astype(BF16), centred(values).astype(BF16),
                           preferred_element_type=F32)

        ahead = first_dot(0)
        for v in range(LEV):
            covar = ahead
            if v + 1 < LEV:
                ahead = first_dot(v + 1)
            rows = slice(v * MEMBERS, (v + 1) * MEMBERS)
            tapered = (covar * horiz[slot, 0:width, :]).astype(BF16)
            state[rows, :] = state[rows, :] + jnp.dot(weight, tapered, preferred_element_type=F32)

    most = counts[0]
    for b in range(1, NB):
        most = jnp.maximum(most, counts[b])

    def straight(width):
        for b in range(NB):
            regress(b % 2, width, *column_step(b))
        out[...] = state[...].astype(BF16)

    for low_width, width in ((-1, 128), (128, 160)):
        @pl.when((most > low_width) & (most <= width))
        def _(width=width):
            straight(width)

    @pl.when(most > 160)
    def _():
        for b in range(NB):
            devs[b], weights[b], gcols[b], levels[b] = column_step(b)

        def batch(b, carry):
            regress(0, OBS, devs[b], weights[b], gcols[b], levels[b])
            return carry
        lax.fori_loop(0, NB, batch, 0)
        out[...] = state[...].astype(BF16)


def update(x, obs, perturbed, ghi, glo, obs_tile, obs_column, obs_level, tapers):
    vmem = pl.BlockSpec(memory_space=pltpu.VMEM)
    return pl.pallas_call(
        update_kernel,
        out_shape=jax.ShapeDtypeStruct((LEV * MEMBERS, COLS), BF16),
        in_specs=[vmem] * (8 + NB - 1),
        out_specs=vmem,
        scratch_shapes=[
            pltpu.VMEM((LEV * MEMBERS, COLS), F32),
            pltpu.VMEM((MEMBERS, NB * OBS), F32),
            pltpu.VMEM((NB, OBS, MEMBERS), F32),
            pltpu.VMEM((NB, MEMBERS, OBS), BF16),
            pltpu.VMEM((NB, OBS, 128), F32),
            pltpu.VMEM((NB, OBS, 128), F32),
            pltpu.VMEM((2, OBS, COLS), F32),
            pltpu.SMEM((NB,), jnp.int32),
        ],
        compiler_params=pltpu.CompilerParams(vmem_limit_bytes=28 * 1024 * 1024),
        name="update",
    )(x, obs, perturbed, ghi, glo, obs_tile, obs_column, obs_level, *tapers)


def per_device(ensemble, perturbed, factor, obs_tile, obs_column, obs_level):
    x = ensemble.transpose(1, 0, 2).reshape(LEV * MEMBERS, COLS)
    obs, ghi, glo, *tapers = exchange(x, obs_tile, obs_column, obs_level, factor)
    posterior = update(x, obs, perturbed, ghi, glo, obs_tile, obs_column, obs_level, tapers)
    return posterior.reshape(LEV, MEMBERS, COLS).transpose(1, 0, 2)


def solution(mesh):
    return jax.shard_map(
        per_device,
        mesh=mesh,
        in_specs=(P(None, "lev", "tile"), P(), P(), P(), P(), P()),
        out_specs=P(None, "lev", "tile"),
        check_vma=False,
    )
```

```python
import jax
import jax.numpy as jnp
from jax import lax
from jax.experimental import pallas as pl
from jax.experimental.pallas import tpu as pltpu
from jax.sharding import PartitionSpec as P

MEMBERS = 80
OBS = 256
NB = 8
COLS = 1024
LEV = 6
COLUMNS = 32768
RADIUS = 2560
VREACH = 12
TILES = 32
NEAR = -(-RADIUS // COLS)

HALF = 80
PIECE = 5
PLANE = 16
PARTS = ((0, 3), (3, 2))
DEPTH = 8

F32 = jnp.float32
BF16 = jnp.bfloat16


def down(row):
    return jnp.broadcast_to(row, (128, OBS)).T


def inverse_of(value):
    rough = pl.reciprocal(value, approx=True)
    return rough * (2.0 - value * rough)


def exchange_kernel(ens_h, tile_h, col_h, lev_h, fac_h, *refs):
    (obs_out, ghi_out, glo_out), refs = refs[:3], refs[3:]
    taper_out, refs = refs[:NB - 1], refs[NB - 1:]
    exchange_body((ens_h, tile_h, col_h, lev_h, fac_h), obs_out, ghi_out, glo_out, taper_out, *refs)


def exchange_body(given, obs_out, ghi_out, glo_out, taper_out,
                  ens, tile_r, col_r, lev_r, fac, load, buf, r0, s0, r1, s1, r2, s2, full,
                  send0, recv0, send1, recv1, send2, recv2, send3, recv3, send4, recv4):
    t = lax.axis_index("tile")
    l = lax.axis_index("lev")
    core = t % 2
    z_lo = (t // 2) % 4
    x = t // 8
    y = l // 2
    z_hi = l % 2
    plane = x * 4 + y
    z = z_hi * 4 + z_lo

    def plane_peer(d):
        j = 0
        for bit in (1, 2, 4, 8):
            own = (plane // bit) % 2
            j = j + bit * (1 - own if d & bit else own)
        return j, {"tile": (j // 4) * 8 + z_lo * 2 + core, "lev": (j % 4) * 2 + z_hi}

    def depth_peer(d):
        j = (z + d) % DEPTH
        return j, {"tile": x * 8 + (j % 4) * 2 + core, "lev": y * 2 + j // 4}

    loads = [pltpu.make_async_copy(src, dst, load.at[i])
             for i, (src, dst) in enumerate(zip(given, (ens, tile_r, col_r, lev_r, fac)))]
    for i in (1, 2, 3, 0, 4):
        loads[i].start()

    mate = {"tile": t + 1 - 2 * core, "lev": l}
    peers = [mate] + [plane_peer(d)[1] for d in range(1, PLANE)]
    peers += [depth_peer(d)[1] for d in range(1, DEPTH)]
    barrier = pltpu.get_barrier_semaphore()
    for peer in peers:
        pl.semaphore_signal(barrier, inc=1, device_id=peer, device_id_type=pl.DeviceIdType.MESH)

    for i in range(4):
        loads[i].wait()

    def pick(b, carry):
        owned = tile_r[pl.ds(b, 1), :] == t
        column = jnp.where(owned, col_r[pl.ds(b, 1), :], -1)
        level = lev_r[pl.ds(b, 1), :] - l * LEV
        rows = lax.broadcasted_iota(jnp.int32, (COLS, OBS), 0)
        onehot = jnp.where(rows == column, 1.0, 0.0).astype(BF16)
        got = jnp.dot(ens[...], onehot, preferred_element_type=F32)
        total = jnp.zeros((MEMBERS, OBS), F32)
        for v in range(LEV):
            total = total + jnp.where(level == v, got[v * MEMBERS:(v + 1) * MEMBERS], 0.0)
        for h in range(2):
            for mb in range(10):
                buf[b * 20 + h * 10 + mb] = total[mb * 8:mb * 8 + 8, h * 128:h * 128 + 128]
        return carry

    def group(step):
        return (x // 2 + step) % 2

    def pair_copy(step):
        return pltpu.make_async_remote_copy(
            src_ref=buf.at[pl.ds((1 - core) * HALF + group(step) * 8 * PIECE, 8 * PIECE)],
            dst_ref=r0.at[pl.ds(group(step) * 8 * PIECE, 8 * PIECE)],
            send_sem=send0.at[step], recv_sem=recv0.at[step],
            device_id=mate, device_id_type=pl.DeviceIdType.MESH)

    def remote(src, dst, send, recv, peer):
        c = pltpu.make_async_remote_copy(
            src_ref=src, dst_ref=dst, send_sem=send, recv_sem=recv,
            device_id=peer, device_id_type=pl.DeviceIdType.MESH)
        c.start()
        return c

    spread_out, along, gathered, passed = {}, {}, {}, {}

    def send_part(p, d):
        at, size = PARTS[p]
        j, peer = plane_peer(d)
        spread_out[p, d] = remote(s0.at[j, pl.ds(at, size)], r1.at[d, pl.ds(at, size)],
                                  send1.at[p, d], recv1.at[p, d], peer)

    for step in range(4):
        from_batch = (core if step >= 2 else 1 - core) * 4 + group(step % 2) * 2
        lax.fori_loop(0, 2, lambda i, c, from_batch=from_batch: pick(from_batch + i, c), 0, unroll=True)
        if step == 0:
            pl.semaphore_wait(barrier, len(peers))
        if step < 2:
            pair_copy(step).start()
        else:
            pair_copy(step - 2).wait_recv()
            for d in range((step - 2) * 8, (step - 2) * 8 + 8):
                j, _ = plane_peer(d)
                s0[j] = buf[pl.ds(core * HALF + j * PIECE, PIECE)] + r0[pl.ds(j * PIECE, PIECE)]
                if d:
                    send_part(0, d)
    for d in range(1, PLANE):
        send_part(1, d)

    def plane_sum(p):
        at, size = PARTS[p]
        total = s0[plane, at:at + size]
        for d in range(1, PLANE):
            spread_out[p, d].wait_recv()
            total = total + r1[d, at:at + size]
        s1[at:at + size] = total
        for d in range(1, DEPTH):
            along[p, d] = remote(s1.at[pl.ds(at, size)], r2.at[d, pl.ds(at, size)],
                                 send2.at[p, d], recv2.at[p, d], depth_peer(d)[1])

    def depth_sum(p):
        at, size = PARTS[p]
        total = s1[at:at + size]
        for d in range(1, DEPTH):
            along[p, d].wait_recv()
            total = total + r2[d, at:at + size]
        s2[at:at + size] = total
        place = pl.ds(core * HALF + plane * PIECE + at, size)
        full[place] = total
        for d in range(1, PLANE):
            gathered[p, d] = remote(s2.at[pl.ds(at, size)], full.at[place],
                                    send3.at[p, d], recv3.at[p, d], plane_peer(d)[1])

    loads[4].wait()

    def gram(b, carry):
        f = fac[b]
        f_t = f.T
        hi, hi_t = f.astype(BF16), f_t.astype(BF16)
        lo, lo_t = (f - hi.astype(F32)).astype(BF16), (f_t - hi_t.astype(F32)).astype(BF16)
        g = (jnp.dot(hi_t, hi, preferred_element_type=F32)
             + (jnp.dot(hi_t, lo, preferred_element_type=F32)
                + jnp.dot(lo_t, hi, preferred_element_type=F32)))
        g_hi = g.astype(BF16)
        ghi_out[b] = g_hi
        glo_out[b] = (g - g_hi.astype(F32)).astype(BF16)
        return carry
    reach_sq = float(VREACH * VREACH)
    inverse = 1.0 / (MEMBERS - 1)

    def tapers_of(b):
        gcol_d = down((tile_r[b:b + 1, :] * COLS + col_r[b:b + 1, :]).astype(F32))
        level_d = down(lev_r[b:b + 1, :].astype(F32))

        def later(b2, carry):
            g2 = (tile_r[pl.ds(b2, 1), :] * COLS + col_r[pl.ds(b2, 1), :]).astype(F32)
            l2 = lev_r[pl.ds(b2, 1), :].astype(F32)
            for h in range(2):
                cut = slice(h * 128, h * 128 + 128)
                dist = jnp.abs(gcol_d - g2[:, cut])
                dist = jnp.minimum(dist, COLUMNS - dist)
                taper = jnp.maximum(0.0, 1.0 - dist * (1.0 / RADIUS))
                off = level_d - l2[:, cut]
                vert = (reach_sq * inverse) * inverse_of(reach_sq + off * off)
                place = pl.multiple_of((b2 - b - 1) * OBS + h * 128, 128)
                taper_out[b][:, pl.ds(place, 128)] = taper * vert
            return carry
        lax.fori_loop(b + 1, NB, later, 0)

    lax.fori_loop(0, NB, gram, 0, unroll=2)
    plane_sum(0)
    tapers_of(0)
    plane_sum(1)
    tapers_of(1)
    tapers_of(2)
    depth_sum(0)
    tapers_of(3)
    depth_sum(1)
    for b in range(4, NB - 1):
        tapers_of(b)
    for step in range(2):
        pair_copy(step).wait_send()
    for sent in (spread_out, along):
        for c in sent.values():
            c.wait_send()
    for d in range(PLANE):
        j, _ = plane_peer(d)
        if d:
            for p in range(2):
                gathered[p, d].wait_recv()
        part = full.at[pl.ds(core * HALF + j * PIECE, PIECE)]
        passed[d] = remote(part, part, send4.at[d], recv4.at[d], mate)

    def unpack(cb, carry):
        for mb in range(10):
            obs_out[mb * 8:mb * 8 + 8, pl.ds(pl.multiple_of(cb * 128, 128), 128)] = full[cb * 10 + mb]
        return carry
    lax.fori_loop(core * 8, core * 8 + 8, unpack, 0)
    for c in gathered.values():
        c.wait_send()
    for d in range(PLANE):
        passed[d].wait_recv()
    lax.fori_loop(8 - core * 8, 16 - core * 8, unpack, 0)
    for d in range(PLANE):
        passed[d].wait_send()


def exchange(ensemble, obs_tile, obs_column, obs_level, factor):
    vmem = pl.BlockSpec(memory_space=pltpu.VMEM)
    dma = pltpu.SemaphoreType.DMA
    piece = (PIECE, 8, 128)
    return pl.pallas_call(
        exchange_kernel,
        out_shape=(
            jax.ShapeDtypeStruct((MEMBERS, NB * OBS), F32),
            jax.ShapeDtypeStruct((NB, OBS, OBS), BF16),
            jax.ShapeDtypeStruct((NB, OBS, OBS), BF16),
        ) + tuple(jax.ShapeDtypeStruct((OBS, (NB - 1 - b) * OBS), F32) for b in range(NB - 1)),
        in_specs=[pl.BlockSpec(memory_space=pltpu.HBM)] * 5,
        out_specs=(vmem,) * (NB + 2),
        scratch_shapes=[
            pltpu.VMEM((LEV * MEMBERS, COLS), BF16),
            pltpu.VMEM((NB, OBS), jnp.int32),
            pltpu.VMEM((NB, OBS), jnp.int32),
            pltpu.VMEM((NB, OBS), jnp.int32),
            pltpu.VMEM((NB, OBS, OBS), F32),
            dma((5,)),
            pltpu.VMEM((2 * HALF, 8, 128), F32),
            pltpu.VMEM((HALF, 8, 128), F32),
            pltpu.VMEM((PLANE,) + piece, F32),
            pltpu.VMEM((PLANE,) + piece, F32),
            pltpu.VMEM(piece, F32),
            pltpu.VMEM((DEPTH,) + piece, F32),
            pltpu.VMEM(piece, F32),
            pltpu.VMEM((2 * HALF, 8, 128), F32),
            dma((2,)), dma((2,)), dma((2, PLANE)), dma((2, PLANE)),
            dma((2, DEPTH)), dma((2, DEPTH)),
            dma((2, PLANE)), dma((2, PLANE)), dma((PLANE,)), dma((PLANE,)),
        ],
        compiler_params=pltpu.CompilerParams(
            collective_id=0, has_side_effects=True, vmem_limit_bytes=14 * 1024 * 1024),
        name="exchange",
    )(*(pltpu.with_memory_space_constraint(a, pltpu.HBM)
        for a in (ensemble, obs_tile, obs_column, obs_level, factor)))


def centred(values):
    return values - jnp.sum(values, axis=0, keepdims=True) * (1.0 / MEMBERS)


def update_kernel(x_ref, obs_ref, pert, ghi, glo, tile_r, col_r, lev_r, *refs):
    tapers = refs[:NB - 1]
    out, state, aug, devs, weights, gcols, levels, horiz, counts = refs[NB - 1:]
    t = lax.axis_index("tile")
    first = lax.axis_index("lev") * LEV
    state[...] = x_ref[...].astype(F32)
    aug[...] = obs_ref[...]
    reach_sq = float(VREACH * VREACH)
    inverse = 1.0 / (MEMBERS - 1)

    low = (t + TILES - NEAR) % TILES
    turns = []
    for b in range(NB):
        owner = tile_r[b:b + 1, :]
        rel = owner - low
        rel = jnp.where(rel < 0, rel + TILES, rel)
        counts[b] = jnp.sum(jnp.where(rel < 2 * NEAR + 1, 1.0, 0.0)).astype(jnp.int32)
        skipped = jnp.sum(jnp.where(owner < low, 1.0, 0.0)).astype(jnp.int32)
        turns.append(lax.rem(OBS - skipped, OBS))

    def column_step(b):
        priors = aug[:, b * OBS:(b + 1) * OBS]
        prior_dev = centred(priors)
        innovation = pert[b] - priors
        in_hi = innovation.astype(BF16)
        in_lo = (innovation - in_hi.astype(F32)).astype(BF16)
        g_hi = ghi[b]
        full_weight = (jnp.dot(in_hi, g_hi, preferred_element_type=F32)
                       + jnp.dot(in_lo, g_hi, preferred_element_type=F32)
                       + jnp.dot(in_hi, glo[b], preferred_element_type=F32))
        if b + 1 < NB:
            rest = slice((b + 1) * OBS, NB * OBS)
            values = aug[:, rest]
            covar = jnp.dot(prior_dev.T.astype(BF16), centred(values).astype(BF16),
                            preferred_element_type=F32)
            tapered = (covar * tapers[b][...]).astype(BF16)
            aug[:, rest] = values + jnp.dot(full_weight.astype(BF16), tapered,
                                            preferred_element_type=F32)
        dev_t = pltpu.roll(prior_dev, turns[b], 1).T
        weight = pltpu.roll(full_weight, turns[b], 1).astype(BF16)
        gcol = (tile_r[b:b + 1, :] * COLS + col_r[b:b + 1, :]).astype(F32)
        gcol_d = pltpu.roll(jnp.broadcast_to(gcol, (128, OBS)), turns[b], 1).T
        lev = lev_r[b:b + 1, :].astype(F32)
        level_d = pltpu.roll(jnp.broadcast_to(lev, (128, OBS)), turns[b], 1).T
        return dev_t, weight, gcol_d, level_d

    def regress(slot, width, dev_t, weight, gcol_d, level_d):
        lanes = lax.broadcasted_iota(jnp.int32, (width, 128), 1)
        for q in range(COLS // 128):
            dist = jnp.abs(gcol_d[0:width] - (t * COLS + q * 128 + lanes).astype(F32))
            dist = jnp.minimum(dist, COLUMNS - dist)
            horiz[slot, 0:width, q * 128:q * 128 + 128] = jnp.maximum(0.0, 1.0 - dist * (1.0 / RADIUS))
        weight = weight[:, 0:width]
        level_d = level_d[0:width, 0:MEMBERS]
        dev_t = dev_t[0:width]

        def first_dot(v):
            off = level_d - (first + v).astype(F32)
            vert = (reach_sq * inverse) * inverse_of(reach_sq + off * off)
            values = state[v * MEMBERS:(v + 1) * MEMBERS, :]
            return jnp.dot((dev_t * vert).astype(BF16), centred(values).astype(BF16),
                           preferred_element_type=F32)

        ahead = first_dot(0)
        for v in range(LEV):
            covar = ahead
            if v + 1 < LEV:
                ahead = first_dot(v + 1)
            rows = slice(v * MEMBERS, (v + 1) * MEMBERS)
            tapered = (covar * horiz[slot, 0:width, :]).astype(BF16)
            state[rows, :] = state[rows, :] + jnp.dot(weight, tapered, preferred_element_type=F32)

    most = counts[0]
    for b in range(1, NB):
        most = jnp.maximum(most, counts[b])

    def straight(width):
        for b in range(NB):
            regress(b % 2, width, *column_step(b))
        out[...] = state[...].astype(BF16)

    for low_width, width in ((-1, 128), (128, 160)):
        @pl.when((most > low_width) & (most <= width))
        def _(width=width):
            straight(width)

    @pl.when(most > 160)
    def _():
        for b in range(NB):
            devs[b], weights[b], gcols[b], levels[b] = column_step(b)

        def batch(b, carry):
            regress(0, OBS, devs[b], weights[b], gcols[b], levels[b])
            return carry
        lax.fori_loop(0, NB, batch, 0)
        out[...] = state[...].astype(BF16)


def update(x, obs, perturbed, ghi, glo, obs_tile, obs_column, obs_level, tapers):
    vmem = pl.BlockSpec(memory_space=pltpu.VMEM)
    return pl.pallas_call(
        update_kernel,
        out_shape=jax.ShapeDtypeStruct((LEV * MEMBERS, COLS), BF16),
        in_specs=[vmem] * (8 + NB - 1),
        out_specs=vmem,
        scratch_shapes=[
            pltpu.VMEM((LEV * MEMBERS, COLS), F32),
            pltpu.VMEM((MEMBERS, NB * OBS), F32),
            pltpu.VMEM((NB, OBS, MEMBERS), F32),
            pltpu.VMEM((NB, MEMBERS, OBS), BF16),
            pltpu.VMEM((NB, OBS, 128), F32),
            pltpu.VMEM((NB, OBS, 128), F32),
            pltpu.VMEM((2, OBS, COLS), F32),
            pltpu.SMEM((NB,), jnp.int32),
        ],
        compiler_params=pltpu.CompilerParams(vmem_limit_bytes=28 * 1024 * 1024),
        name="update",
    )(x, obs, perturbed, ghi, glo, obs_tile, obs_column, obs_level, *tapers)


def per_device(ensemble, perturbed, factor, obs_tile, obs_column, obs_level):
    x = ensemble.transpose(1, 0, 2).reshape(LEV * MEMBERS, COLS)
    obs, ghi, glo, *tapers = exchange(x, obs_tile, obs_column, obs_level, factor)
    posterior = update(x, obs, perturbed, ghi, glo, obs_tile, obs_column, obs_level, tapers)
    return posterior.reshape(LEV, MEMBERS, COLS).transpose(1, 0, 2)


def solution(mesh):
    return jax.shard_map(
        per_device,
        mesh=mesh,
        in_specs=(P(None, "lev", "tile"), P(), P(), P(), P(), P()),
        out_specs=P(None, "lev", "tile"),
        check_vma=False,
    )
```

```python
import jax
import jax.numpy as jnp
from jax import lax
from jax.experimental import pallas as pl
from jax.experimental.pallas import tpu as pltpu
from jax.sharding import PartitionSpec as P

MEMBERS = 80
OBS = 256
NB = 8
COLS = 1024
LEV = 6
COLUMNS = 32768
RADIUS = 2560
VREACH = 12
TILES = 32
NEAR = -(-RADIUS // COLS)

HALF = 80
PIECE = 5
PLANE = 16
PARTS = ((0, 3), (3, 2))
DEPTH = 8

F32 = jnp.float32
BF16 = jnp.bfloat16


def down(row):
    return jnp.broadcast_to(row, (128, OBS)).T


def inverse_of(value):
    rough = pl.reciprocal(value, approx=True)
    return rough * (2.0 - value * rough)


def exchange_kernel(ens_h, tile_h, col_h, lev_h, fac_h, *refs):
    (obs_out, ghi_out, glo_out), refs = refs[:3], refs[3:]
    taper_out, refs = refs[:NB - 1], refs[NB - 1:]
    exchange_body((ens_h, tile_h, col_h, lev_h, fac_h), obs_out, ghi_out, glo_out, taper_out, *refs)


def exchange_body(given, obs_out, ghi_out, glo_out, taper_out,
                  ens, tile_r, col_r, lev_r, fac, load, buf, r0, s0, r1, s1, r2, s2, full,
                  send0, recv0, send1, recv1, send2, recv2, send3, recv3, send4, recv4):
    t = lax.axis_index("tile")
    l = lax.axis_index("lev")
    core = t % 2
    z_lo = (t // 2) % 4
    x = t // 8
    y = l // 2
    z_hi = l % 2
    plane = x * 4 + y
    z = z_hi * 4 + z_lo

    def plane_peer(d):
        j = (plane + d) % PLANE
        return j, {"tile": (j // 4) * 8 + z_lo * 2 + core, "lev": (j % 4) * 2 + z_hi}

    def depth_peer(d):
        j = (z + d) % DEPTH
        return j, {"tile": x * 8 + (j % 4) * 2 + core, "lev": y * 2 + j // 4}

    loads = [pltpu.make_async_copy(src, dst, load.at[i])
             for i, (src, dst) in enumerate(zip(given, (ens, tile_r, col_r, lev_r, fac)))]
    for i in (1, 2, 3, 0, 4):
        loads[i].start()

    mate = {"tile": t + 1 - 2 * core, "lev": l}
    peers = [mate] + [plane_peer(d)[1] for d in range(1, PLANE)]
    peers += [depth_peer(d)[1] for d in range(1, DEPTH)]
    barrier = pltpu.get_barrier_semaphore()
    for peer in peers:
        pl.semaphore_signal(barrier, inc=1, device_id=peer, device_id_type=pl.DeviceIdType.MESH)

    for i in range(4):
        loads[i].wait()

    def pick(b, carry):
        owned = tile_r[pl.ds(b, 1), :] == t
        column = jnp.where(owned, col_r[pl.ds(b, 1), :], -1)
        level = lev_r[pl.ds(b, 1), :] - l * LEV
        rows = lax.broadcasted_iota(jnp.int32, (COLS, OBS), 0)
        onehot = jnp.where(rows == column, 1.0, 0.0).astype(BF16)
        got = jnp.dot(ens[...], onehot, preferred_element_type=F32)
        total = jnp.zeros((MEMBERS, OBS), F32)
        for v in range(LEV):
            total = total + jnp.where(level == v, got[v * MEMBERS:(v + 1) * MEMBERS], 0.0)
        for h in range(2):
            for mb in range(10):
                buf[b * 20 + h * 10 + mb] = total[mb * 8:mb * 8 + 8, h * 128:h * 128 + 128]
        return carry

    def pair_copy(step):
        return pltpu.make_async_remote_copy(
            src_ref=buf.at[pl.ds((1 - core) * HALF + step * 8 * PIECE, 8 * PIECE)],
            dst_ref=r0.at[pl.ds(step * 8 * PIECE, 8 * PIECE)],
            send_sem=send0.at[step], recv_sem=recv0.at[step],
            device_id=mate, device_id_type=pl.DeviceIdType.MESH)

    for step in range(4):
        from_batch = (step * 2 + 4 * (1 - core)) % NB
        lax.fori_loop(0, 2, lambda i, c, from_batch=from_batch: pick(from_batch + i, c), 0, unroll=True)
        if step == 0:
            pl.semaphore_wait(barrier, len(peers))
        if step < 2:
            pair_copy(step).start()

    order = list(range(1, PLANE)) + [0]
    def remote(src, dst, send, recv, peer):
        c = pltpu.make_async_remote_copy(
            src_ref=src, dst_ref=dst, send_sem=send, recv_sem=recv,
            device_id=peer, device_id_type=pl.DeviceIdType.MESH)
        c.start()
        return c

    spread_out, along, gathered, passed = {}, {}, {}, {}
    for step in range(2):
        pair_copy(step).wait_recv()
    for p, (at, size) in enumerate(PARTS):
        for d in order:
            j, peer = plane_peer(d)
            if p == 0:
                s0[j] = buf[pl.ds(core * HALF + j * PIECE, PIECE)] + r0[pl.ds(j * PIECE, PIECE)]
            if d:
                spread_out[p, d] = remote(s0.at[j, pl.ds(at, size)], r1.at[d, pl.ds(at, size)],
                                          send1.at[p, d], recv1.at[p, d], peer)

    def plane_sum(p):
        at, size = PARTS[p]
        total = s0[plane, at:at + size]
        for d in range(1, PLANE):
            spread_out[p, d].wait_recv()
            total = total + r1[d, at:at + size]
        s1[at:at + size] = total
        for d in range(1, DEPTH):
            along[p, d] = remote(s1.at[pl.ds(at, size)], r2.at[d, pl.ds(at, size)],
                                 send2.at[p, d], recv2.at[p, d], depth_peer(d)[1])

    def depth_sum(p):
        at, size = PARTS[p]
        total = s1[at:at + size]
        for d in range(1, DEPTH):
            along[p, d].wait_recv()
            total = total + r2[d, at:at + size]
        s2[at:at + size] = total
        place = pl.ds(core * HALF + plane * PIECE + at, size)
        full[place] = total
        for d in range(1, PLANE):
            gathered[p, d] = remote(s2.at[pl.ds(at, size)], full.at[place],
                                    send3.at[p, d], recv3.at[p, d], plane_peer(d)[1])

    loads[4].wait()

    def gram(b, carry):
        f = fac[b]
        f_t = f.T
        hi, hi_t = f.astype(BF16), f_t.astype(BF16)
        lo, lo_t = (f - hi.astype(F32)).astype(BF16), (f_t - hi_t.astype(F32)).astype(BF16)
        g = (jnp.dot(hi_t, hi, preferred_element_type=F32)
             + (jnp.dot(hi_t, lo, preferred_element_type=F32)
                + jnp.dot(lo_t, hi, preferred_element_type=F32)))
        g_hi = g.astype(BF16)
        ghi_out[b] = g_hi
        glo_out[b] = (g - g_hi.astype(F32)).astype(BF16)
        return carry
    reach_sq = float(VREACH * VREACH)
    inverse = 1.0 / (MEMBERS - 1)

    def tapers_of(b):
        gcol_d = down((tile_r[b:b + 1, :] * COLS + col_r[b:b + 1, :]).astype(F32))
        level_d = down(lev_r[b:b + 1, :].astype(F32))

        def later(b2, carry):
            g2 = (tile_r[pl.ds(b2, 1), :] * COLS + col_r[pl.ds(b2, 1), :]).astype(F32)
            l2 = lev_r[pl.ds(b2, 1), :].astype(F32)
            for h in range(2):
                cut = slice(h * 128, h * 128 + 128)
                dist = jnp.abs(gcol_d - g2[:, cut])
                dist = jnp.minimum(dist, COLUMNS - dist)
                taper = jnp.maximum(0.0, 1.0 - dist * (1.0 / RADIUS))
                off = level_d - l2[:, cut]
                vert = (reach_sq * inverse) * inverse_of(reach_sq + off * off)
                place = pl.multiple_of((b2 - b - 1) * OBS + h * 128, 128)
                taper_out[b][:, pl.ds(place, 128)] = taper * vert
            return carry
        lax.fori_loop(b + 1, NB, later, 0)

    lax.fori_loop(0, NB // 2, gram, 0, unroll=2)
    plane_sum(0)
    lax.fori_loop(NB // 2, NB, gram, 0, unroll=2)
    plane_sum(1)
    tapers_of(0)
    tapers_of(1)
    depth_sum(0)
    tapers_of(2)
    depth_sum(1)
    for b in range(3, NB - 1):
        tapers_of(b)
    for step in range(2):
        pair_copy(step).wait_send()
    for sent in (spread_out, along):
        for c in sent.values():
            c.wait_send()
    for d in range(PLANE):
        j = (plane - d + PLANE) % PLANE
        if d:
            for p in range(2):
                gathered[p, d].wait_recv()
        part = full.at[pl.ds(core * HALF + j * PIECE, PIECE)]
        passed[d] = remote(part, part, send4.at[d], recv4.at[d], mate)

    def unpack(cb, carry):
        for mb in range(10):
            obs_out[mb * 8:mb * 8 + 8, pl.ds(pl.multiple_of(cb * 128, 128), 128)] = full[cb * 10 + mb]
        return carry
    lax.fori_loop(core * 8, core * 8 + 8, unpack, 0)
    for c in gathered.values():
        c.wait_send()
    for d in range(PLANE):
        passed[d].wait_recv()
    lax.fori_loop(8 - core * 8, 16 - core * 8, unpack, 0)
    for d in range(PLANE):
        passed[d].wait_send()


def exchange(ensemble, obs_tile, obs_column, obs_level, factor):
    vmem = pl.BlockSpec(memory_space=pltpu.VMEM)
    dma = pltpu.SemaphoreType.DMA
    piece = (PIECE, 8, 128)
    return pl.pallas_call(
        exchange_kernel,
        out_shape=(
            jax.ShapeDtypeStruct((MEMBERS, NB * OBS), F32),
            jax.ShapeDtypeStruct((NB, OBS, OBS), BF16),
            jax.ShapeDtypeStruct((NB, OBS, OBS), BF16),
        ) + tuple(jax.ShapeDtypeStruct((OBS, (NB - 1 - b) * OBS), F32) for b in range(NB - 1)),
        in_specs=[pl.BlockSpec(memory_space=pltpu.HBM)] * 5,
        out_specs=(vmem,) * (NB + 2),
        scratch_shapes=[
            pltpu.VMEM((LEV * MEMBERS, COLS), BF16),
            pltpu.VMEM((NB, OBS), jnp.int32),
            pltpu.VMEM((NB, OBS), jnp.int32),
            pltpu.VMEM((NB, OBS), jnp.int32),
            pltpu.VMEM((NB, OBS, OBS), F32),
            dma((5,)),
            pltpu.VMEM((2 * HALF, 8, 128), F32),
            pltpu.VMEM((HALF, 8, 128), F32),
            pltpu.VMEM((PLANE,) + piece, F32),
            pltpu.VMEM((PLANE,) + piece, F32),
            pltpu.VMEM(piece, F32),
            pltpu.VMEM((DEPTH,) + piece, F32),
            pltpu.VMEM(piece, F32),
            pltpu.VMEM((2 * HALF, 8, 128), F32),
            dma((2,)), dma((2,)), dma((2, PLANE)), dma((2, PLANE)),
            dma((2, DEPTH)), dma((2, DEPTH)),
            dma((2, PLANE)), dma((2, PLANE)), dma((PLANE,)), dma((PLANE,)),
        ],
        compiler_params=pltpu.CompilerParams(
            collective_id=0, has_side_effects=True, vmem_limit_bytes=14 * 1024 * 1024),
        name="exchange",
    )(*(pltpu.with_memory_space_constraint(a, pltpu.HBM)
        for a in (ensemble, obs_tile, obs_column, obs_level, factor)))


def centred(values):
    return values - jnp.sum(values, axis=0, keepdims=True) * (1.0 / MEMBERS)


def update_kernel(x_ref, obs_ref, pert, ghi, glo, tile_r, col_r, lev_r, *refs):
    tapers = refs[:NB - 1]
    out, state, aug, devs, weights, gcols, levels, horiz, counts = refs[NB - 1:]
    t = lax.axis_index("tile")
    first = lax.axis_index("lev") * LEV
    state[...] = x_ref[...].astype(F32)
    aug[...] = obs_ref[...]
    reach_sq = float(VREACH * VREACH)
    inverse = 1.0 / (MEMBERS - 1)

    low = (t + TILES - NEAR) % TILES
    turns = []
    for b in range(NB):
        owner = tile_r[b:b + 1, :]
        rel = owner - low
        rel = jnp.where(rel < 0, rel + TILES, rel)
        counts[b] = jnp.sum(jnp.where(rel < 2 * NEAR + 1, 1.0, 0.0)).astype(jnp.int32)
        skipped = jnp.sum(jnp.where(owner < low, 1.0, 0.0)).astype(jnp.int32)
        turns.append(lax.rem(OBS - skipped, OBS))

    def column_step(b):
        priors = aug[:, b * OBS:(b + 1) * OBS]
        prior_dev = centred(priors)
        innovation = pert[b] - priors
        in_hi = innovation.astype(BF16)
        in_lo = (innovation - in_hi.astype(F32)).astype(BF16)
        g_hi = ghi[b]
        full_weight = (jnp.dot(in_hi, g_hi, preferred_element_type=F32)
                       + jnp.dot(in_lo, g_hi, preferred_element_type=F32)
                       + jnp.dot(in_hi, glo[b], preferred_element_type=F32))
        if b + 1 < NB:
            rest = slice((b + 1) * OBS, NB * OBS)
            values = aug[:, rest]
            covar = jnp.dot(prior_dev.T.astype(BF16), centred(values).astype(BF16),
                            preferred_element_type=F32)
            tapered = (covar * tapers[b][...]).astype(BF16)
            aug[:, rest] = values + jnp.dot(full_weight.astype(BF16), tapered,
                                            preferred_element_type=F32)
        dev_t = pltpu.roll(prior_dev, turns[b], 1).T
        weight = pltpu.roll(full_weight, turns[b], 1).astype(BF16)
        gcol = (tile_r[b:b + 1, :] * COLS + col_r[b:b + 1, :]).astype(F32)
        gcol_d = pltpu.roll(jnp.broadcast_to(gcol, (128, OBS)), turns[b], 1).T
        lev = lev_r[b:b + 1, :].astype(F32)
        level_d = pltpu.roll(jnp.broadcast_to(lev, (128, OBS)), turns[b], 1).T
        return dev_t, weight, gcol_d, level_d

    def regress(slot, width, dev_t, weight, gcol_d, level_d):
        lanes = lax.broadcasted_iota(jnp.int32, (width, 128), 1)
        for q in range(COLS // 128):
            dist = jnp.abs(gcol_d[0:width] - (t * COLS + q * 128 + lanes).astype(F32))
            dist = jnp.minimum(dist, COLUMNS - dist)
            horiz[slot, 0:width, q * 128:q * 128 + 128] = jnp.maximum(0.0, 1.0 - dist * (1.0 / RADIUS))
        weight = weight[:, 0:width]
        level_d = level_d[0:width, 0:MEMBERS]
        dev_t = dev_t[0:width]

        def first_dot(v):
            off = level_d - (first + v).astype(F32)
            vert = (reach_sq * inverse) * inverse_of(reach_sq + off * off)
            values = state[v * MEMBERS:(v + 1) * MEMBERS, :]
            return jnp.dot((dev_t * vert).astype(BF16), centred(values).astype(BF16),
                           preferred_element_type=F32)

        ahead = first_dot(0)
        for v in range(LEV):
            covar = ahead
            if v + 1 < LEV:
                ahead = first_dot(v + 1)
            rows = slice(v * MEMBERS, (v + 1) * MEMBERS)
            tapered = (covar * horiz[slot, 0:width, :]).astype(BF16)
            state[rows, :] = state[rows, :] + jnp.dot(weight, tapered, preferred_element_type=F32)

    most = counts[0]
    for b in range(1, NB):
        most = jnp.maximum(most, counts[b])

    def straight(width):
        for b in range(NB):
            regress(b % 2, width, *column_step(b))
        out[...] = state[...].astype(BF16)

    for low_width, width in ((-1, 128), (128, 160)):
        @pl.when((most > low_width) & (most <= width))
        def _(width=width):
            straight(width)

    @pl.when(most > 160)
    def _():
        for b in range(NB):
            devs[b], weights[b], gcols[b], levels[b] = column_step(b)

        def batch(b, carry):
            regress(0, OBS, devs[b], weights[b], gcols[b], levels[b])
            return carry
        lax.fori_loop(0, NB, batch, 0)
        out[...] = state[...].astype(BF16)


def update(x, obs, perturbed, ghi, glo, obs_tile, obs_column, obs_level, tapers):
    vmem = pl.BlockSpec(memory_space=pltpu.VMEM)
    return pl.pallas_call(
        update_kernel,
        out_shape=jax.ShapeDtypeStruct((LEV * MEMBERS, COLS), BF16),
        in_specs=[vmem] * (8 + NB - 1),
        out_specs=vmem,
        scratch_shapes=[
            pltpu.VMEM((LEV * MEMBERS, COLS), F32),
            pltpu.VMEM((MEMBERS, NB * OBS), F32),
            pltpu.VMEM((NB, OBS, MEMBERS), F32),
            pltpu.VMEM((NB, MEMBERS, OBS), BF16),
            pltpu.VMEM((NB, OBS, 128), F32),
            pltpu.VMEM((NB, OBS, 128), F32),
            pltpu.VMEM((2, OBS, COLS), F32),
            pltpu.SMEM((NB,), jnp.int32),
        ],
        compiler_params=pltpu.CompilerParams(vmem_limit_bytes=28 * 1024 * 1024),
        name="update",
    )(x, obs, perturbed, ghi, glo, obs_tile, obs_column, obs_level, *tapers)


def per_device(ensemble, perturbed, factor, obs_tile, obs_column, obs_level):
    x = ensemble.transpose(1, 0, 2).reshape(LEV * MEMBERS, COLS)
    obs, ghi, glo, *tapers = exchange(x, obs_tile, obs_column, obs_level, factor)
    posterior = update(x, obs, perturbed, ghi, glo, obs_tile, obs_column, obs_level, tapers)
    return posterior.reshape(LEV, MEMBERS, COLS).transpose(1, 0, 2)


def solution(mesh):
    return jax.shard_map(
        per_device,
        mesh=mesh,
        in_specs=(P(None, "lev", "tile"), P(), P(), P(), P(), P()),
        out_specs=P(None, "lev", "tile"),
        check_vma=False,
    )
```

```python
import jax
import jax.numpy as jnp
from jax import lax
from jax.experimental import pallas as pl
from jax.experimental.pallas import tpu as pltpu
from jax.sharding import PartitionSpec as P

MEMBERS = 80
OBS = 256
NB = 8
COLS = 1024
LEV = 6
COLUMNS = 32768
RADIUS = 2560
VREACH = 12
TILES = 32
NEAR = -(-RADIUS // COLS)

HALF = 80
PIECE = 5
PLANE = 16
PARTS = ((0, 3), (3, 2))
DEPTH = 8

F32 = jnp.float32
BF16 = jnp.bfloat16


def down(row):
    return jnp.broadcast_to(row, (128, OBS)).T


def inverse_of(value):
    rough = pl.reciprocal(value, approx=True)
    return rough * (2.0 - value * rough)


def exchange_kernel(ens_h, tile_h, col_h, lev_h, fac_h, *refs):
    (obs_out, ghi_out, glo_out), refs = refs[:3], refs[3:]
    taper_out, refs = refs[:NB - 1], refs[NB - 1:]
    exchange_body((ens_h, tile_h, col_h, lev_h, fac_h), obs_out, ghi_out, glo_out, taper_out, *refs)


def exchange_body(given, obs_out, ghi_out, glo_out, taper_out,
                  ens, tile_r, col_r, lev_r, fac, load, buf, r0, s0, r1, s1, r2, s2, full,
                  send0, recv0, send1, recv1, send2, recv2, send3, recv3, send4, recv4):
    t = lax.axis_index("tile")
    l = lax.axis_index("lev")
    core = t % 2
    z_lo = (t // 2) % 4
    x = t // 8
    y = l // 2
    z_hi = l % 2
    plane = x * 4 + y
    z = z_hi * 4 + z_lo

    def plane_peer(d):
        j = (plane + d) % PLANE
        return j, {"tile": (j // 4) * 8 + z_lo * 2 + core, "lev": (j % 4) * 2 + z_hi}

    def depth_peer(d):
        j = (z + d) % DEPTH
        return j, {"tile": x * 8 + (j % 4) * 2 + core, "lev": y * 2 + j // 4}

    loads = [pltpu.make_async_copy(src, dst, load.at[i])
             for i, (src, dst) in enumerate(zip(given, (ens, tile_r, col_r, lev_r, fac)))]
    for i in (1, 2, 3, 0, 4):
        loads[i].start()

    mate = {"tile": t + 1 - 2 * core, "lev": l}
    peers = [mate] + [plane_peer(d)[1] for d in range(1, PLANE)]
    peers += [depth_peer(d)[1] for d in range(1, DEPTH)]
    barrier = pltpu.get_barrier_semaphore()
    for peer in peers:
        pl.semaphore_signal(barrier, inc=1, device_id=peer, device_id_type=pl.DeviceIdType.MESH)

    for i in range(4):
        loads[i].wait()

    def pick(b, carry):
        owned = tile_r[pl.ds(b, 1), :] == t
        column = jnp.where(owned, col_r[pl.ds(b, 1), :], -1)
        level = lev_r[pl.ds(b, 1), :] - l * LEV
        rows = lax.broadcasted_iota(jnp.int32, (COLS, OBS), 0)
        onehot = jnp.where(rows == column, 1.0, 0.0).astype(BF16)
        got = jnp.dot(ens[...], onehot, preferred_element_type=F32)
        total = jnp.zeros((MEMBERS, OBS), F32)
        for v in range(LEV):
            total = total + jnp.where(level == v, got[v * MEMBERS:(v + 1) * MEMBERS], 0.0)
        for h in range(2):
            for mb in range(10):
                buf[b * 20 + h * 10 + mb] = total[mb * 8:mb * 8 + 8, h * 128:h * 128 + 128]
        return carry

    def pair_copy(step):
        return pltpu.make_async_remote_copy(
            src_ref=buf.at[pl.ds((1 - core) * HALF + step * 8 * PIECE, 8 * PIECE)],
            dst_ref=r0.at[pl.ds(step * 8 * PIECE, 8 * PIECE)],
            send_sem=send0.at[step], recv_sem=recv0.at[step],
            device_id=mate, device_id_type=pl.DeviceIdType.MESH)

    for step in range(4):
        from_batch = (step * 2 + 4 * (1 - core)) % NB
        lax.fori_loop(0, 2, lambda i, c, from_batch=from_batch: pick(from_batch + i, c), 0, unroll=True)
        if step == 0:
            pl.semaphore_wait(barrier, len(peers))
        if step < 2:
            pair_copy(step).start()

    order = list(range(1, PLANE)) + [0]
    def remote(src, dst, send, recv, peer):
        c = pltpu.make_async_remote_copy(
            src_ref=src, dst_ref=dst, send_sem=send, recv_sem=recv,
            device_id=peer, device_id_type=pl.DeviceIdType.MESH)
        c.start()
        return c

    spread_out, along, gathered, passed = {}, {}, {}, {}
    for step in range(2):
        pair_copy(step).wait_recv()
    for p, (at, size) in enumerate(PARTS):
        for d in order:
            j, peer = plane_peer(d)
            if p == 0:
                s0[j] = buf[pl.ds(core * HALF + j * PIECE, PIECE)] + r0[pl.ds(j * PIECE, PIECE)]
            if d:
                spread_out[p, d] = remote(s0.at[j, pl.ds(at, size)], r1.at[d, pl.ds(at, size)],
                                          send1.at[p, d], recv1.at[p, d], peer)

    def plane_sum(p):
        at, size = PARTS[p]
        total = s0[plane, at:at + size]
        for d in range(1, PLANE):
            spread_out[p, d].wait_recv()
            total = total + r1[d, at:at + size]
        s1[at:at + size] = total
        for d in range(1, DEPTH):
            along[p, d] = remote(s1.at[pl.ds(at, size)], r2.at[d, pl.ds(at, size)],
                                 send2.at[p, d], recv2.at[p, d], depth_peer(d)[1])

    def depth_sum(p):
        at, size = PARTS[p]
        total = s1[at:at + size]
        for d in range(1, DEPTH):
            along[p, d].wait_recv()
            total = total + r2[d, at:at + size]
        s2[at:at + size] = total
        place = pl.ds(core * HALF + plane * PIECE + at, size)
        full[place] = total
        for d in range(1, PLANE):
            gathered[p, d] = remote(s2.at[pl.ds(at, size)], full.at[place],
                                    send3.at[p, d], recv3.at[p, d], plane_peer(d)[1])

    loads[4].wait()

    def gram(b, carry):
        f = fac[b]
        f_t = f.T
        hi, hi_t = f.astype(BF16), f_t.astype(BF16)
        lo, lo_t = (f - hi.astype(F32)).astype(BF16), (f_t - hi_t.astype(F32)).astype(BF16)
        g = (jnp.dot(hi_t, hi, preferred_element_type=F32)
             + (jnp.dot(hi_t, lo, preferred_element_type=F32)
                + jnp.dot(lo_t, hi, preferred_element_type=F32)))
        g_hi = g.astype(BF16)
        ghi_out[b] = g_hi
        glo_out[b] = (g - g_hi.astype(F32)).astype(BF16)
        return carry
    reach_sq = float(VREACH * VREACH)
    inverse = 1.0 / (MEMBERS - 1)

    def tapers_of(b):
        gcol_d = down((tile_r[b:b + 1, :] * COLS + col_r[b:b + 1, :]).astype(F32))
        level_d = down(lev_r[b:b + 1, :].astype(F32))

        def later(b2, carry):
            g2 = (tile_r[pl.ds(b2, 1), :] * COLS + col_r[pl.ds(b2, 1), :]).astype(F32)
            l2 = lev_r[pl.ds(b2, 1), :].astype(F32)
            for h in range(2):
                cut = slice(h * 128, h * 128 + 128)
                dist = jnp.abs(gcol_d - g2[:, cut])
                dist = jnp.minimum(dist, COLUMNS - dist)
                taper = jnp.maximum(0.0, 1.0 - dist * (1.0 / RADIUS))
                off = level_d - l2[:, cut]
                vert = (reach_sq * inverse) * inverse_of(reach_sq + off * off)
                place = pl.multiple_of((b2 - b - 1) * OBS + h * 128, 128)
                taper_out[b][:, pl.ds(place, 128)] = taper * vert
            return carry
        lax.fori_loop(b + 1, NB, later, 0)

    lax.fori_loop(0, NB, gram, 0, unroll=2)
    plane_sum(0)
    tapers_of(0)
    plane_sum(1)
    tapers_of(1)
    tapers_of(2)
    depth_sum(0)
    tapers_of(3)
    depth_sum(1)
    for b in range(4, NB - 1):
        tapers_of(b)
    for step in range(2):
        pair_copy(step).wait_send()
    for sent in (spread_out, along):
        for c in sent.values():
            c.wait_send()
    for d in range(PLANE):
        j = (plane - d + PLANE) % PLANE
        if d:
            for p in range(2):
                gathered[p, d].wait_recv()
        part = full.at[pl.ds(core * HALF + j * PIECE, PIECE)]
        passed[d] = remote(part, part, send4.at[d], recv4.at[d], mate)

    def unpack(cb, carry):
        for mb in range(10):
            obs_out[mb * 8:mb * 8 + 8, pl.ds(pl.multiple_of(cb * 128, 128), 128)] = full[cb * 10 + mb]
        return carry
    lax.fori_loop(core * 8, core * 8 + 8, unpack, 0)
    for c in gathered.values():
        c.wait_send()
    for d in range(PLANE):
        passed[d].wait_recv()
    lax.fori_loop(8 - core * 8, 16 - core * 8, unpack, 0)
    for d in range(PLANE):
        passed[d].wait_send()


def exchange(ensemble, obs_tile, obs_column, obs_level, factor):
    vmem = pl.BlockSpec(memory_space=pltpu.VMEM)
    dma = pltpu.SemaphoreType.DMA
    piece = (PIECE, 8, 128)
    return pl.pallas_call(
        exchange_kernel,
        out_shape=(
            jax.ShapeDtypeStruct((MEMBERS, NB * OBS), F32),
            jax.ShapeDtypeStruct((NB, OBS, OBS), BF16),
            jax.ShapeDtypeStruct((NB, OBS, OBS), BF16),
        ) + tuple(jax.ShapeDtypeStruct((OBS, (NB - 1 - b) * OBS), F32) for b in range(NB - 1)),
        in_specs=[pl.BlockSpec(memory_space=pltpu.HBM)] * 5,
        out_specs=(vmem,) * (NB + 2),
        scratch_shapes=[
            pltpu.VMEM((LEV * MEMBERS, COLS), BF16),
            pltpu.VMEM((NB, OBS), jnp.int32),
            pltpu.VMEM((NB, OBS), jnp.int32),
            pltpu.VMEM((NB, OBS), jnp.int32),
            pltpu.VMEM((NB, OBS, OBS), F32),
            dma((5,)),
            pltpu.VMEM((2 * HALF, 8, 128), F32),
            pltpu.VMEM((HALF, 8, 128), F32),
            pltpu.VMEM((PLANE,) + piece, F32),
            pltpu.VMEM((PLANE,) + piece, F32),
            pltpu.VMEM(piece, F32),
            pltpu.VMEM((DEPTH,) + piece, F32),
            pltpu.VMEM(piece, F32),
            pltpu.VMEM((2 * HALF, 8, 128), F32),
            dma((2,)), dma((2,)), dma((2, PLANE)), dma((2, PLANE)),
            dma((2, DEPTH)), dma((2, DEPTH)),
            dma((2, PLANE)), dma((2, PLANE)), dma((PLANE,)), dma((PLANE,)),
        ],
        compiler_params=pltpu.CompilerParams(
            collective_id=0, has_side_effects=True, vmem_limit_bytes=14 * 1024 * 1024),
        name="exchange",
    )(*(pltpu.with_memory_space_constraint(a, pltpu.HBM)
        for a in (ensemble, obs_tile, obs_column, obs_level, factor)))


def centred(values):
    return values - jnp.sum(values, axis=0, keepdims=True) * (1.0 / MEMBERS)


def update_kernel(x_ref, obs_ref, pert, ghi, glo, tile_r, col_r, lev_r, *refs):
    tapers = refs[:NB - 1]
    out, state, aug, devs, weights, gcols, levels, horiz, counts = refs[NB - 1:]
    t = lax.axis_index("tile")
    first = lax.axis_index("lev") * LEV
    state[...] = x_ref[...].astype(F32)
    aug[...] = obs_ref[...]
    reach_sq = float(VREACH * VREACH)
    inverse = 1.0 / (MEMBERS - 1)

    low = (t + TILES - NEAR) % TILES
    turns = []
    for b in range(NB):
        owner = tile_r[b:b + 1, :]
        rel = owner - low
        rel = jnp.where(rel < 0, rel + TILES, rel)
        counts[b] = jnp.sum(jnp.where(rel < 2 * NEAR + 1, 1.0, 0.0)).astype(jnp.int32)
        skipped = jnp.sum(jnp.where(owner < low, 1.0, 0.0)).astype(jnp.int32)
        turns.append(lax.rem(OBS - skipped, OBS))

    def column_step(b):
        priors = aug[:, b * OBS:(b + 1) * OBS]
        prior_dev = centred(priors)
        innovation = pert[b] - priors
        in_hi = innovation.astype(BF16)
        in_lo = (innovation - in_hi.astype(F32)).astype(BF16)
        g_hi = ghi[b]
        both = jnp.dot(jnp.concatenate([in_hi, in_lo], axis=0), g_hi, preferred_element_type=F32)
        full_weight = (both[0:MEMBERS] + both[MEMBERS:2 * MEMBERS]
                       + jnp.dot(in_hi, glo[b], preferred_element_type=F32))
        if b + 1 < NB:
            rest = slice((b + 1) * OBS, NB * OBS)
            values = aug[:, rest]
            covar = jnp.dot(prior_dev.T.astype(BF16), centred(values).astype(BF16),
                            preferred_element_type=F32)
            tapered = (covar * tapers[b][...]).astype(BF16)
            aug[:, rest] = values + jnp.dot(full_weight.astype(BF16), tapered,
                                            preferred_element_type=F32)
        dev_t = pltpu.roll(prior_dev, turns[b], 1).T
        weight = pltpu.roll(full_weight, turns[b], 1).astype(BF16)
        gcol = (tile_r[b:b + 1, :] * COLS + col_r[b:b + 1, :]).astype(F32)
        gcol_d = pltpu.roll(jnp.broadcast_to(gcol, (128, OBS)), turns[b], 1).T
        lev = lev_r[b:b + 1, :].astype(F32)
        level_d = pltpu.roll(jnp.broadcast_to(lev, (128, OBS)), turns[b], 1).T
        return dev_t, weight, gcol_d, level_d

    def regress(slot, width, dev_t, weight, gcol_d, level_d):
        lanes = lax.broadcasted_iota(jnp.int32, (width, 128), 1)
        offset = gcol_d[0:width] - (t * COLS).astype(F32)
        offset = jnp.where(offset > COLUMNS / 2 + COLS / 2, offset - COLUMNS, offset)
        offset = jnp.where(offset < COLS / 2 - COLUMNS / 2, offset + COLUMNS, offset)
        for q in range(COLS // 128):
            dist = jnp.abs(offset - (q * 128 + lanes).astype(F32))
            horiz[slot, 0:width, q * 128:q * 128 + 128] = jnp.maximum(0.0, 1.0 - dist * (1.0 / RADIUS))
        weight = weight[:, 0:width]
        level_d = level_d[0:width, 0:MEMBERS]
        dev_t = dev_t[0:width]

        def first_dot(v):
            off = level_d - (first + v).astype(F32)
            vert = (reach_sq * inverse) * inverse_of(reach_sq + off * off)
            values = state[v * MEMBERS:(v + 1) * MEMBERS, :]
            return jnp.dot((dev_t * vert).astype(BF16), centred(values).astype(BF16),
                           preferred_element_type=F32)

        ahead = first_dot(0)
        for v in range(LEV):
            covar = ahead
            if v + 1 < LEV:
                ahead = first_dot(v + 1)
            rows = slice(v * MEMBERS, (v + 1) * MEMBERS)
            tapered = (covar * horiz[slot, 0:width, :]).astype(BF16)
            state[rows, :] = state[rows, :] + jnp.dot(weight, tapered, preferred_element_type=F32)

    most = counts[0]
    for b in range(1, NB):
        most = jnp.maximum(most, counts[b])

    def straight(width):
        for b in range(NB):
            regress(b % 2, width, *column_step(b))
        out[...] = state[...].astype(BF16)

    for low_width, width in ((-1, 128), (128, 160)):
        @pl.when((most > low_width) & (most <= width))
        def _(width=width):
            straight(width)

    @pl.when(most > 160)
    def _():
        for b in range(NB):
            devs[b], weights[b], gcols[b], levels[b] = column_step(b)

        def batch(b, carry):
            regress(0, OBS, devs[b], weights[b], gcols[b], levels[b])
            return carry
        lax.fori_loop(0, NB, batch, 0)
        out[...] = state[...].astype(BF16)


def update(x, obs, perturbed, ghi, glo, obs_tile, obs_column, obs_level, tapers):
    vmem = pl.BlockSpec(memory_space=pltpu.VMEM)
    return pl.pallas_call(
        update_kernel,
        out_shape=jax.ShapeDtypeStruct((LEV * MEMBERS, COLS), BF16),
        in_specs=[vmem] * (8 + NB - 1),
        out_specs=vmem,
        scratch_shapes=[
            pltpu.VMEM((LEV * MEMBERS, COLS), F32),
            pltpu.VMEM((MEMBERS, NB * OBS), F32),
            pltpu.VMEM((NB, OBS, MEMBERS), F32),
            pltpu.VMEM((NB, MEMBERS, OBS), BF16),
            pltpu.VMEM((NB, OBS, 128), F32),
            pltpu.VMEM((NB, OBS, 128), F32),
            pltpu.VMEM((2, OBS, COLS), F32),
            pltpu.SMEM((NB,), jnp.int32),
        ],
        compiler_params=pltpu.CompilerParams(vmem_limit_bytes=28 * 1024 * 1024),
        name="update",
    )(x, obs, perturbed, ghi, glo, obs_tile, obs_column, obs_level, *tapers)


def per_device(ensemble, perturbed, factor, obs_tile, obs_column, obs_level):
    x = ensemble.transpose(1, 0, 2).reshape(LEV * MEMBERS, COLS)
    obs, ghi, glo, *tapers = exchange(x, obs_tile, obs_column, obs_level, factor)
    posterior = update(x, obs, perturbed, ghi, glo, obs_tile, obs_column, obs_level, tapers)
    return posterior.reshape(LEV, MEMBERS, COLS).transpose(1, 0, 2)


def solution(mesh):
    return jax.shard_map(
        per_device,
        mesh=mesh,
        in_specs=(P(None, "lev", "tile"), P(), P(), P(), P(), P()),
        out_specs=P(None, "lev", "tile"),
        check_vma=False,
    )
```
